128 devices in a mesh: wide: 32 (over y, z, core), narrow: 4 (over x).
Axes of the slice: x: 4, y: 4, z: 4, core: 2. Of those that a mesh axis runs over, the one named last changes fastest.
Arguments:
- traces: bfloat16 [32, 4, 64, 24, 512], P('wide', 'narrow'), may hold values from -6 to 6
- pair_first: int32 [32, 4, 9, 32], P('wide', 'narrow'), may hold values from 0 to 63
- pair_second: int32 [32, 4, 9, 32], P('wide', 'narrow'), may hold values from 0 to 63
- pair_valid: int32 [32, 4, 9, 32], P('wide', 'narrow'), may hold values from 0 to 1, as said below
Outputs:
- corr_sum: float32 [32, 4, 64, 24, 256], P('wide', 'narrow')
The draws below stay inside these ranges and needn't reach their ends.
Inputs may be any that keep to these rules, and one draw needn't show every extreme that they name: `pair_valid`: 0 in every direction that points outside the grid of cells; slot 0 of every direction inside the grid is 1; cells differ in the share of live slots.
All inputs are finite; a program needn't handle non-finite values.
Results may differ from the reference program's by a relative error of at most 0.0003.
Values may be sent and summed in bfloat16 or wider, within the bound.
A program may use at most 256 MiB of HBM per device.

```python
import math
import jax
import jax.numpy as jnp
from jax import lax

C = 24
S = 512
LAGS = 256
DIRS = 9
EV_DEV = 64
BP = 32
NFFT = 640
CELL_ROWS = 32
CELL_COLS = 4


def draw_pair_valid(key, part):
    key = jax.random.fold_in(key, 7)
    density_key, slot_key = jax.random.split(key)
    row_ids = jnp.arange(CELL_ROWS, dtype=jnp.int32)[:, None, None, None]
    col_ids = jnp.arange(CELL_COLS, dtype=jnp.int32)[None, :, None, None]
    heading = jnp.arange(DIRS, dtype=jnp.int32)[None, None, :, None]
    slot_ids = jnp.arange(BP, dtype=jnp.int32)[None, None, None, :]
    row_step = heading // 3 - 1
    col_step = heading % 3 - 1
    inside = (row_ids + row_step >= 0) & (row_ids + row_step < CELL_ROWS) & (col_ids + col_step >= 0) & (col_ids + col_step < CELL_COLS)
    density = jax.random.randint(density_key, (CELL_ROWS, CELL_COLS, 1, 1), 3, 11)
    tenths = jax.random.randint(slot_key, (CELL_ROWS, CELL_COLS, DIRS, BP), 0, 10)
    live = (tenths < density) | (slot_ids == 0)
    return (inside & live).astype(jnp.int32)


def place_ends(drawn, key, low, high):
    longest = drawn.shape.index(max(drawn.shape))
    spots = []
    for shift in (0, 1):
        where = [jax.random.randint(jax.random.fold_in(key, axis), (), 0, length) for axis, length in enumerate(drawn.shape)]
        where[longest] = (where[longest] + shift) % drawn.shape[longest]
        spots.append(tuple(where))
    return drawn.at[spots[0]].set(low).at[spots[1]].set(high)


def block_levels(rng, extent, shards, least, largest):
    level = 1.0
    for dim, parts in shards:
        heights = jax.random.uniform(jax.random.fold_in(jax.random.fold_in(rng, 6), dim), (parts,), jnp.float32, least / len(shards), largest / len(shards))
        level = level * jnp.repeat(jnp.exp(heights), extent[dim] // parts).reshape((-1,) + (1,) * (len(extent) - 1 - dim))
    return level


def bell_draw(rng, shape, width, most, shards=(), held_as=jnp.bfloat16):
    level = block_levels(rng, shape, shards, -0.22, 0.18) if shards else 1.0
    drawn = jax.random.normal(rng, shape, jnp.float32) * width * level
    return jnp.minimum(jnp.maximum(drawn, -most), most).astype(held_as)


def setup_inputs(seed: int = 0) -> dict:
    key_of = jax.random.split(jax.random.key(seed), 5)
    return {
        "traces": bell_draw(key_of[0], (CELL_ROWS, CELL_COLS, EV_DEV, C, S), 1.0, 6.0, ((0, 32), (1, 4))),
        "pair_first": place_ends(jax.random.randint(key_of[1], (CELL_ROWS, CELL_COLS, DIRS, BP), 0, EV_DEV), jax.random.fold_in(key_of[1], 1), 0, EV_DEV - 1).astype(jnp.int32),
        "pair_second": place_ends(jax.random.randint(key_of[2], (CELL_ROWS, CELL_COLS, DIRS, BP), 0, EV_DEV), jax.random.fold_in(key_of[2], 1), 0, EV_DEV - 1).astype(jnp.int32),
        "pair_valid": draw_pair_valid(jax.random.fold_in(key_of[4], 71), 0),
    }


def make_tables(samples, nfft, lags):
    half_bins = nfft // 2
    half_lags = lags // 2
    angle_step = 2.0 * math.pi / nfft
    sample_ids = jnp.arange(samples, dtype=jnp.int32)
    bin_ids = jnp.arange(half_bins, dtype=jnp.int32)
    phase = (sample_ids[:, None] * bin_ids[None, :] % nfft).astype(jnp.float32) * angle_step
    alternate = (1 - 2 * (sample_ids % 2)).astype(jnp.float32)
    sine_part = jnp.where(bin_ids[None, :] == 0, alternate[:, None], -jnp.sin(phase))
    forward_table = jnp.concatenate([jnp.cos(phase), sine_part], axis=1)
    lag_ids = jnp.arange(lags, dtype=jnp.int32) - half_lags
    lag_phase = (bin_ids[:, None] * lag_ids[None, :] % nfft).astype(jnp.float32) * angle_step
    weights = jnp.where(bin_ids == 0, 1.0, 2.0).astype(jnp.float32)[:, None]
    scale_factor = 1.0 / (nfft * math.sqrt(samples))
    sign_row = (1 - 2 * (lag_ids % 2)).astype(jnp.float32)[None, :]
    cos_rows = weights * jnp.cos(lag_phase) * scale_factor
    sin_ahead = jnp.where(bin_ids[:, None] == 0, sign_row, -2.0 * jnp.sin(lag_phase)) * scale_factor
    sin_behind = jnp.where(bin_ids[:, None] == 0, sign_row, 2.0 * jnp.sin(lag_phase)) * scale_factor
    inverse_table = jnp.concatenate([cos_rows, sin_ahead], axis=0)
    reverse_table = jnp.concatenate([cos_rows, sin_behind], axis=0)
    return (forward_table, inverse_table, reverse_table)

def cross_spectrum(first, second):
    half_bins = first.shape[-1] // 2
    first_re = first[..., :half_bins]
    first_im = first[..., half_bins:]
    second_re = second[..., :half_bins]
    second_im = second[..., half_bins:]
    beyond_zero = (jnp.arange(half_bins) > 0).astype(first.dtype)
    real_part = first_re * second_re + beyond_zero * first_im * second_im
    imag_part = beyond_zero * (first_re * second_im - first_im * second_re) + (1 - beyond_zero) * first_im * second_im
    return jnp.concatenate([real_part, imag_part], axis=-1)

def reference(traces, pair_first, pair_second, pair_valid):
    row_count, col_count, events, channels, samples = traces.shape
    forward_table, inverse_table, reverse_table = make_tables(samples, NFFT, LAGS)
    signal = traces.reshape(-1, samples).astype(jnp.float32)
    spectra = jnp.dot(signal, forward_table, precision=lax.Precision.HIGHEST).reshape(-1, channels, NFFT)
    total = row_count * col_count * events
    ahead_sum = jnp.zeros((total, channels, NFFT), jnp.float32)
    behind_sum = jnp.zeros((total, channels, NFFT), jnp.float32)
    row_ids = jnp.arange(row_count, dtype=jnp.int32)[:, None, None]
    col_ids = jnp.arange(col_count, dtype=jnp.int32)[None, :, None]
    for heading in range(9):
        row_step = heading // 3 - 1
        col_step = heading % 3 - 1
        near_row = jnp.clip(row_ids + row_step, 0, row_count - 1)
        near_col = jnp.clip(col_ids + col_step, 0, col_count - 1)
        first_index = ((row_ids * col_count + col_ids) * events + pair_first[:, :, heading, :]).reshape(-1)
        second_index = ((near_row * col_count + near_col) * events + pair_second[:, :, heading, :]).reshape(-1)
        live_mask = pair_valid[:, :, heading, :].reshape(-1).astype(jnp.float32)
        products = cross_spectrum(spectra[first_index], spectra[second_index]) * live_mask[:, None, None]
        ahead_sum = ahead_sum.at[first_index].add(products)
        behind_sum = behind_sum.at[second_index].add(products)
    result = jnp.dot(ahead_sum.reshape(-1, NFFT), inverse_table, precision=lax.Precision.HIGHEST)
    result = result + jnp.dot(behind_sum.reshape(-1, NFFT), reverse_table, precision=lax.Precision.HIGHEST)
    return result.reshape(row_count, col_count, events, channels, LAGS)
```

```python
import functools
import math

import jax
import jax.numpy as jnp
import ml_dtypes
import numpy as np
from jax import lax
from jax.experimental import pallas as pl
from jax.experimental.pallas import tpu as pltpu
from jax.sharding import PartitionSpec as P

LAGS = 256
NFFT = 768
BLOCKS = 3
BINS = 128
CHUNK = 2
LAG = 2
WINDOW = 3
MESH = pl.DeviceIdType.MESH
F32 = jnp.float32
BF16 = jnp.bfloat16


def split_np(table):
    high = table.astype(ml_dtypes.bfloat16)
    low = (table - high.astype(np.float64)).astype(ml_dtypes.bfloat16)
    return np.stack([high, low])


def make_tables(samples):
    freq = np.arange(NFFT // 2, dtype=np.float64) + 0.5
    step = 2.0 * math.pi / NFFT
    phase = np.arange(samples, dtype=np.float64)[:, None] * freq[None, :] * step
    parts = []
    for b in range(BLOCKS):
        cols = slice(b * BINS, (b + 1) * BINS)
        parts += [np.cos(phase[:, cols]), -np.sin(phase[:, cols])]
    forward = np.concatenate(parts, axis=1)
    lag = np.arange(LAGS, dtype=np.float64) - LAGS // 2
    phase = freq[:, None] * lag[None, :] * step
    scale = 2.0 / (NFFT * math.sqrt(samples))
    parts = []
    for b in range(BLOCKS):
        rows = slice(b * BINS, (b + 1) * BINS)
        parts += [np.cos(phase[rows]) * scale, -np.sin(phase[rows]) * scale]
    return split_np(forward), split_np(np.concatenate(parts, axis=0))


def split(v):
    high = v.astype(BF16)
    return high, (v - high.astype(F32)).astype(BF16)


def dot(a, b):
    return jnp.dot(a, b, preferred_element_type=F32)


def kernel(
    traces, first, second, valid, fwd_hbm, inv_hbm, out,
    raw, wide32, cells, part_up, part_own, part_down, got_up, got_down,
    weights, codes, fwd, inv, held,
    load_sem, table_sem, code_send, code_recv,
    x_send_left, x_send_right, x_from_left, x_from_right,
    y_send_up, y_send_down, y_from_up, y_from_down, out_sem,
):
    events, channels, samples = traces.shape
    lanes = samples // 128
    chunks = channels // CHUNK
    rows, cols = lax.axis_size("wide"), lax.axis_size("narrow")
    row, col = lax.axis_index("wide"), lax.axis_index("narrow")
    left = {"narrow": lax.rem(col + cols - 1, cols)}
    right = {"narrow": lax.rem(col + 1, cols)}
    up = {"wide": lax.rem(row + rows - 1, rows)}
    down = {"wide": lax.rem(row + 1, rows)}

    load = pltpu.make_async_copy(traces, raw, load_sem)
    load.start()
    load_fwd = pltpu.make_async_copy(fwd_hbm, fwd, table_sem.at[0])
    load_inv = pltpu.make_async_copy(inv_hbm, inv, table_sem.at[1])
    load_fwd.start()
    load_inv.start()

    barrier = pltpu.get_barrier_semaphore()
    for peer in (left, right, up, down):
        pl.semaphore_signal(barrier, inc=1, device_id=peer, device_id_type=MESH)

    slots = first.shape[1]
    codes[0, 0:9, 0:slots] = jnp.where(
        valid[...] == 1, first[...] * events + second[...], -1
    )
    pl.semaphore_wait(barrier, 4)

    def remote(src, dst, send, recv, peer):
        return pltpu.make_async_remote_copy(
            src_ref=src, dst_ref=dst, send_sem=send, recv_sem=recv,
            device_id=peer, device_id_type=MESH,
        )

    code_copies = [
        remote(codes.at[0], codes.at[slot], code_send.at[slot - 1], code_recv.at[slot - 1], peer)
        for slot, peer in ((1, right), (2, left), (3, down), (4, up))
    ]
    for copy in code_copies:
        copy.start()

    def x_left(k):
        block = pl.ds(k * CHUNK, CHUNK)
        return remote(
            cells.at[block, events : 2 * events, :], cells.at[block, 2 * events : 3 * events, :],
            x_send_left.at[k], x_from_right.at[k], left,
        )

    def x_right(k):
        block = pl.ds(k * CHUNK, CHUNK)
        return remote(
            cells.at[block, events : 2 * events, :], cells.at[block, 0:events, :],
            x_send_right.at[k], x_from_left.at[k], right,
        )

    def y_up(k):
        block = pl.ds(k * CHUNK, CHUNK)
        return remote(
            part_up.at[block], got_down.at[block], y_send_up.at[k], y_from_down.at[k], up
        )

    def y_down(k):
        block = pl.ds(k * CHUNK, CHUNK)
        return remote(
            part_down.at[block], got_up.at[block], y_send_down.at[k], y_from_up.at[k], down
        )

    load.wait()
    for i in range(lanes):
        spread = raw[:, :, i * 128 : (i + 1) * 128].astype(F32)
        wide32[i] = spread.reshape(events * channels, 128)

    def turn(k, _):
        for n in range(CHUNK):
            c = k * CHUNK + n
            for i in range(lanes):
                lane_block = wide32[i, pl.ds(c, events, stride=channels), :]
                cells[c, events : 2 * events, i * 128 : (i + 1) * 128] = lane_block.astype(BF16)

        @pl.when(k < WINDOW)
        def _():
            x_left(k).start()
            x_right(k).start()

        return 0

    lax.fori_loop(0, chunks, turn, 0)

    for copy in code_copies:
        copy.wait()

    ids = lax.broadcasted_iota(jnp.int32, (events, slots), 0)

    def ends(slot, heading):
        code = codes[slot, heading : heading + 1, 0:slots]
        live = code >= 0
        head = jnp.where(live, code // events, -1)
        tail = jnp.where(live, code % events, -1)
        return (
            jnp.where(ids == head, 1.0, 0.0).astype(BF16),
            jnp.where(ids == tail, 1.0, 0.0).astype(BF16),
        )

    def outer(a, b):
        return lax.dot_general(
            a, b, (((1,), (1,)), ((), ())), preferred_element_type=F32
        )

    for i in (-1, 0, 1):
        target = {-1: 3, 0: 0, 1: 4}[i]
        for j in (-1, 0, 1):
            source = {-1: 1, 0: 0, 1: 2}[j]
            head, tail = ends(target, (1 - i) * 3 + (j + 1))
            count = outer(head, tail)
            head, tail = ends(source, (i + 1) * 3 + (1 - j))
            count = count + outer(tail, head)
            weights[
                (i + 1) * events : (i + 2) * events, (j + 1) * events : (j + 2) * events
            ] = count.astype(BF16)

    load_fwd.wait()
    load_inv.wait()

    def gather(k):
        x_left(k).wait()
        x_right(k).wait()

        @pl.when(k + WINDOW < chunks)
        def _():
            x_left(k + WINDOW).start()
            x_right(k + WINDOW).start()

        for n in range(CHUNK):
            c = k * CHUNK + n
            part = dot(weights[...], cells[c])
            part_up[c] = part[0:events]
            part_own[c] = part[events : 2 * events]
            part_down[c] = part[2 * events : 3 * events]
        y_up(k).start()
        y_down(k).start()

    def correlate(k):
        y_up(k).wait()
        y_down(k).wait()
        size = CHUNK * events
        block = pl.ds(k * CHUNK, CHUNK)
        x = cells[block, events : 2 * events, :].reshape(size, samples)
        y = (part_own[block] + got_up[block] + got_down[block]).reshape(size, samples)
        y_high, y_low = split(y)
        stack3 = jnp.concatenate([x, y_high, y_low], axis=0)
        stack2 = jnp.concatenate([x, y_high], axis=0)
        total = jnp.zeros((size, LAGS), F32)
        for b in range(BLOCKS):
            span = slice(b * 2 * BINS, (b + 1) * 2 * BINS)
            coarse = dot(stack3, fwd[0, :, span])
            fine = dot(stack2, fwd[1, :, span])
            xs = coarse[0:size] + fine[0:size]
            ys = coarse[size : 2 * size] + coarse[2 * size :] + fine[size:]
            xr, xi = xs[:, :BINS], xs[:, BINS:]
            yr, yi = ys[:, :BINS], ys[:, BINS:]
            s = jnp.concatenate([xr * yr + xi * yi, xr * yi - xi * yr], axis=1)
            s_high, s_low = split(s)
            both = dot(jnp.concatenate([s_high, s_low], axis=0), inv[0, span, :])
            total = total + (both[:size] + both[size:] + dot(s_high, inv[1, span, :]))
        for n in range(CHUNK):
            for i in range(LAGS // 128):
                held[i, pl.ds(k * CHUNK + n, events, stride=channels), :] = total[
                    n * events : (n + 1) * events, i * 128 : (i + 1) * 128
                ]

    def step(k, _):
        @pl.when(k < chunks)
        def _():
            gather(k)

        @pl.when(k >= LAG)
        def _():
            correlate(k - LAG)

        return 0

    lax.fori_loop(0, chunks + LAG, step, 0)
    stores = [
        pltpu.make_async_copy(held.at[i], out.at[:, i * 128 : (i + 1) * 128], out_sem.at[i])
        for i in range(LAGS // 128)
    ]
    for store in stores:
        store.start()
    for store in stores:
        store.wait()


def local(forward, inverse, traces, pair_first, pair_second, pair_valid):
    _, _, events, channels, samples = traces.shape
    chunks = channels // CHUNK
    part = pltpu.VMEM((channels, events, samples), F32)
    any_space = pl.BlockSpec(memory_space=pl.ANY)
    in_vmem = pl.BlockSpec(memory_space=pltpu.VMEM)
    dma = pltpu.SemaphoreType.DMA
    out = pl.pallas_call(
        kernel,
        out_shape=jax.ShapeDtypeStruct((events * channels, LAGS), F32),
        in_specs=[any_space, in_vmem, in_vmem, in_vmem, any_space, any_space],
        out_specs=any_space,
        scratch_shapes=[
            pltpu.VMEM((events, channels, samples), BF16),
            pltpu.VMEM((samples // 128, events * channels, 128), F32),
            pltpu.VMEM((channels, 3 * events, samples), BF16),
            part, part, part, part, part,
            pltpu.VMEM((3 * events, 3 * events), BF16),
            pltpu.VMEM((5, 16, 128), jnp.int32),
            pltpu.VMEM(forward.shape, BF16),
            pltpu.VMEM(inverse.shape, BF16),
            pltpu.VMEM((LAGS // 128, events * channels, 128), F32),
            dma, dma((2,)), dma((4,)), dma((4,)),
        ] + [dma((chunks,))] * 8 + [dma((LAGS // 128,))],
        compiler_params=pltpu.CompilerParams(
            collective_id=0, has_side_effects=True, vmem_limit_bytes=56 * 1024 * 1024
        ),
        cost_estimate=pl.CostEstimate(
            flops=8 * 10**9, bytes_accessed=6 * 10**6, transcendentals=0
        ),
        name="event_correlation",
    )(traces[0, 0], pair_first[0, 0], pair_second[0, 0], pair_valid[0, 0], forward, inverse)
    return out.reshape(1, 1, events, channels, LAGS)


def solution(mesh):
    forward, inverse = make_tables(512)
    spec4 = P("wide", "narrow", None, None)
    spec5 = P("wide", "narrow", None, None, None)

    def run(traces, pair_first, pair_second, pair_valid):
        return local(
            jnp.asarray(forward), jnp.asarray(inverse), traces, pair_first, pair_second, pair_valid
        )

    return jax.shard_map(
        run, mesh=mesh, in_specs=(spec5, spec4, spec4, spec4), out_specs=spec5, check_vma=False
    )
```

```python
import functools
import math

import jax
import jax.numpy as jnp
import ml_dtypes
import numpy as np
from jax import lax
from jax.experimental import pallas as pl
from jax.experimental.pallas import tpu as pltpu
from jax.sharding import PartitionSpec as P

LAGS = 256
NFFT = 768
BLOCKS = 3
BINS = 128
CHUNK = 2
LAG = 2
MESH = pl.DeviceIdType.MESH
F32 = jnp.float32
BF16 = jnp.bfloat16


def split_np(table):
    high = table.astype(ml_dtypes.bfloat16)
    low = (table - high.astype(np.float64)).astype(ml_dtypes.bfloat16)
    return np.stack([high, low])


def make_tables(samples):
    freq = np.arange(NFFT // 2, dtype=np.float64) + 0.5
    step = 2.0 * math.pi / NFFT
    phase = np.arange(samples, dtype=np.float64)[:, None] * freq[None, :] * step
    parts = []
    for b in range(BLOCKS):
        cols = slice(b * BINS, (b + 1) * BINS)
        parts += [np.cos(phase[:, cols]), -np.sin(phase[:, cols])]
    forward = np.concatenate(parts, axis=1)
    lag = np.arange(LAGS, dtype=np.float64) - LAGS // 2
    phase = freq[:, None] * lag[None, :] * step
    scale = 2.0 / (NFFT * math.sqrt(samples))
    parts = []
    for b in range(BLOCKS):
        rows = slice(b * BINS, (b + 1) * BINS)
        parts += [np.cos(phase[rows]) * scale, -np.sin(phase[rows]) * scale]
    return split_np(forward), split_np(np.concatenate(parts, axis=0))


def split(v):
    high = v.astype(BF16)
    return high, (v - high.astype(F32)).astype(BF16)


def dot(a, b):
    return jnp.dot(a, b, preferred_element_type=F32)


def kernel(
    traces, first, second, valid, fwd_hbm, inv_hbm, out,
    raw, wide32, cells, part_up, part_own, part_down, got_up, got_down,
    weights, codes, fwd, inv, held,
    load_sem, table_sem, code_send, code_recv,
    x_send_left, x_send_right, x_from_left, x_from_right,
    y_send_up, y_send_down, y_from_up, y_from_down,
):
    events, channels, samples = traces.shape
    lanes = samples // 128
    chunks = channels // CHUNK
    rows, cols = lax.axis_size("wide"), lax.axis_size("narrow")
    row, col = lax.axis_index("wide"), lax.axis_index("narrow")
    left = {"narrow": lax.rem(col + cols - 1, cols)}
    right = {"narrow": lax.rem(col + 1, cols)}
    up = {"wide": lax.rem(row + rows - 1, rows)}
    down = {"wide": lax.rem(row + 1, rows)}
    has_left, has_right = col > 0, col < cols - 1
    has_up, has_down = row > 0, row < rows - 1
    sides = ((has_left, left), (has_right, right), (has_up, up), (has_down, down))

    load = pltpu.make_async_copy(traces, raw, load_sem)
    load.start()
    barrier = pltpu.get_barrier_semaphore()
    for has, peer in sides:
        @pl.when(has)
        def _():
            pl.semaphore_signal(barrier, inc=1, device_id=peer, device_id_type=MESH)

    load_fwd = pltpu.make_async_copy(fwd_hbm, fwd, table_sem.at[0])
    load_inv = pltpu.make_async_copy(inv_hbm, inv, table_sem.at[1])
    load_fwd.start()
    load_inv.start()

    slots = first.shape[2]
    codes[0, 0:9, 0:slots] = jnp.where(
        valid[:, 0, :] == 1, first[:, 0, :] * events + second[:, 0, :], -1
    )

    def blank(has, slot, block, rows_from):
        @pl.when(jnp.logical_not(has))
        def _():
            codes[slot] = jnp.full(codes.shape[1:], -1, jnp.int32)

            def clear(c, _):
                if rows_from is None:
                    block[c] = jnp.zeros(block.shape[1:], block.dtype)
                else:
                    block[c, rows_from : rows_from + events, :] = jnp.zeros(
                        (events, samples), block.dtype
                    )
                return 0

            lax.fori_loop(0, channels, clear, 0)

    blank(has_left, 1, cells, 0)
    blank(has_right, 2, cells, 2 * events)
    blank(has_up, 3, got_up, None)
    blank(has_down, 4, got_down, None)

    def turn(group):
        for i in range(lanes):
            spread = raw[:, group * 8 : (group + 1) * 8, i * 128 : (i + 1) * 128].astype(F32)
            wide32[group, i] = spread.reshape(events * 8, 128)
        for n in range(8):
            for i in range(lanes):
                lane_block = wide32[group, i, pl.ds(n, events, stride=8), :]
                cells[group * 8 + n, events : 2 * events, i * 128 : (i + 1) * 128] = (
                    lane_block.astype(BF16)
                )

    def remote(src, dst, send, recv, peer):
        return pltpu.make_async_remote_copy(
            src_ref=src, dst_ref=dst, send_sem=send, recv_sem=recv,
            device_id=peer, device_id_type=MESH,
        )

    code_copies = [
        remote(codes.at[0], codes.at[slot], code_send.at[slot - 1], code_recv.at[slot - 1], peer)
        for slot, peer in ((2, left), (1, right), (4, up), (3, down))
    ]
    has_from = {1: has_left, 2: has_right, 3: has_up, 4: has_down}

    def x_left(k):
        block = pl.ds(k * CHUNK, CHUNK)
        return remote(
            cells.at[block, events : 2 * events, :], cells.at[block, 2 * events : 3 * events, :],
            x_send_left.at[k], x_from_right.at[k], left,
        )

    def x_right(k):
        block = pl.ds(k * CHUNK, CHUNK)
        return remote(
            cells.at[block, events : 2 * events, :], cells.at[block, 0:events, :],
            x_send_right.at[k], x_from_left.at[k], right,
        )

    def y_up(k):
        block = pl.ds(k * CHUNK, CHUNK)
        return remote(
            part_up.at[block], got_down.at[block], y_send_up.at[k], y_from_down.at[k], up
        )

    def y_down(k):
        block = pl.ds(k * CHUNK, CHUNK)
        return remote(
            part_down.at[block], got_up.at[block], y_send_down.at[k], y_from_up.at[k], down
        )

    def start_if(has, make):
        @pl.when(has)
        def _():
            make().start()

    def wait_send_if(has, make):
        @pl.when(has)
        def _():
            make().wait_send()

    def wait_recv_if(has, make):
        @pl.when(has)
        def _():
            make().wait_recv()

    def send_x(k):
        start_if(has_left, lambda: x_left(k))
        start_if(has_right, lambda: x_right(k))

    load.wait()
    turn(0)
    peers = sum(has.astype(jnp.int32) for has, _ in sides)
    pl.semaphore_wait(barrier, peers)
    for copy, (has, _) in zip(code_copies, sides):
        start_if(has, lambda: copy)
    for k in range(8 // CHUNK):
        send_x(k)
    for group in range(1, channels // 8):
        turn(group)

    for copy, slot, (has, _) in zip(code_copies, (2, 1, 4, 3), sides):
        wait_send_if(has, lambda: copy)
        wait_recv_if(has_from[slot], lambda: copy)

    ids = lax.broadcasted_iota(jnp.int32, (events, slots), 0)

    def ends(slot, heading):
        code = codes[slot, heading : heading + 1, 0:slots]
        live = code >= 0
        head = jnp.where(live, code // events, -1)
        tail = jnp.where(live, code % events, -1)
        return (
            jnp.where(ids == head, 1.0, 0.0).astype(BF16),
            jnp.where(ids == tail, 1.0, 0.0).astype(BF16),
        )

    def outer(a, b):
        return lax.dot_general(
            a, b, (((1,), (1,)), ((), ())), preferred_element_type=F32
        )

    for i in (-1, 0, 1):
        target = {-1: 3, 0: 0, 1: 4}[i]
        for j in (-1, 0, 1):
            source = {-1: 1, 0: 0, 1: 2}[j]
            head, tail = ends(target, (1 - i) * 3 + (j + 1))
            count = outer(head, tail)
            head, tail = ends(source, (i + 1) * 3 + (1 - j))
            count = count + outer(tail, head)
            weights[
                (i + 1) * events : (i + 2) * events, (j + 1) * events : (j + 2) * events
            ] = count.astype(BF16)

    load_fwd.wait()
    load_inv.wait()

    def gather(k):
        @pl.when(k + 8 // CHUNK < chunks)
        def _():
            send_x(k + 8 // CHUNK)

        wait_recv_if(has_left, lambda: x_right(k))
        wait_recv_if(has_right, lambda: x_left(k))

        for n in range(CHUNK):
            c = k * CHUNK + n
            part = dot(weights[...], cells[c])
            part_up[c] = part[0:events]
            part_own[c] = part[events : 2 * events]
            part_down[c] = part[2 * events : 3 * events]
        start_if(has_up, lambda: y_up(k))
        start_if(has_down, lambda: y_down(k))

    def correlate(k):
        wait_recv_if(has_up, lambda: y_down(k))
        wait_recv_if(has_down, lambda: y_up(k))
        size = CHUNK * events
        block = pl.ds(k * CHUNK, CHUNK)
        x = cells[block, events : 2 * events, :].reshape(size, samples)
        y = (part_own[block] + got_up[block] + got_down[block]).reshape(size, samples)
        y_high, y_low = split(y)
        stack3 = jnp.concatenate([x, y_high, y_low], axis=0)
        stack2 = jnp.concatenate([x, y_high], axis=0)
        total = jnp.zeros((size, LAGS), F32)
        for b in range(BLOCKS):
            span = slice(b * 2 * BINS, (b + 1) * 2 * BINS)
            coarse = dot(stack3, fwd[0, :, span])
            fine = dot(stack2, fwd[1, :, span])
            xs = coarse[0:size] + fine[0:size]
            ys = coarse[size : 2 * size] + coarse[2 * size :] + fine[size:]
            xr, xi = xs[:, :BINS], xs[:, BINS:]
            yr, yi = ys[:, :BINS], ys[:, BINS:]
            s = jnp.concatenate([xr * yr + xi * yi, xr * yi - xi * yr], axis=1)
            s_high, s_low = split(s)
            both = dot(jnp.concatenate([s_high, s_low], axis=0), inv[0, span, :])
            total = total + (both[:size] + both[size:] + dot(s_high, inv[1, span, :]))
        per_group = 8 // CHUNK
        for n in range(CHUNK):
            for i in range(LAGS // 128):
                held[i, pl.ds(k % per_group * CHUNK + n, events, stride=8), :] = total[
                    n * events : (n + 1) * events, i * 128 : (i + 1) * 128
                ]

        @pl.when(k % per_group == per_group - 1)
        def _():
            place = pl.ds(pl.multiple_of(k // per_group * 8, 8), 8)
            for i in range(LAGS // 128):
                out[:, place, i * 128 : (i + 1) * 128] = held[i].reshape(events, 8, 128)

    def step(k, _):
        @pl.when(k < chunks)
        def _():
            gather(k)

        @pl.when(k >= LAG)
        def _():
            correlate(k - LAG)

        return 0

    lax.fori_loop(0, chunks + LAG, step, 0)
    def finish(k, _):
        wait_send_if(has_left, lambda: x_left(k))
        wait_send_if(has_right, lambda: x_right(k))
        wait_send_if(has_up, lambda: y_up(k))
        wait_send_if(has_down, lambda: y_down(k))
        return 0

    lax.fori_loop(0, chunks, finish, 0)


def by_heading(pairs):
    return pairs.transpose(0, 2, 1, 3)[0]


def local(forward, inverse, traces, pair_first, pair_second, pair_valid):
    _, _, events, channels, samples = traces.shape
    chunks = channels // CHUNK
    part = pltpu.VMEM((channels, events, samples), F32)
    in_hbm = pl.BlockSpec(memory_space=pltpu.HBM)
    in_vmem = pl.BlockSpec(memory_space=pltpu.VMEM)
    dma = pltpu.SemaphoreType.DMA
    out = pl.pallas_call(
        kernel,
        out_shape=jax.ShapeDtypeStruct((events, channels, LAGS), F32),
        in_specs=[in_hbm, in_vmem, in_vmem, in_vmem, in_hbm, in_hbm],
        out_specs=in_vmem,
        scratch_shapes=[
            pltpu.VMEM((events, channels, samples), BF16),
            pltpu.VMEM((channels // 8, samples // 128, events * 8, 128), F32),
            pltpu.VMEM((channels, 3 * events, samples), BF16),
            part, part, part, part, part,
            pltpu.VMEM((3 * events, 3 * events), BF16),
            pltpu.VMEM((5, 16, 128), jnp.int32),
            pltpu.VMEM(forward.shape, BF16),
            pltpu.VMEM(inverse.shape, BF16),
            pltpu.VMEM((LAGS // 128, events * 8, 128), F32),
            dma, dma((2,)), dma((4,)), dma((4,)),
        ] + [dma((chunks,))] * 8,
        compiler_params=pltpu.CompilerParams(
            collective_id=0, has_side_effects=True, vmem_limit_bytes=40 * 1024 * 1024
        ),
        cost_estimate=pl.CostEstimate(
            flops=8 * 10**9, bytes_accessed=6 * 10**6, transcendentals=0
        ),
        name="event_correlation",
    )(*[pltpu.with_memory_space_constraint(v, pltpu.HBM) for v in (traces[0, 0], by_heading(pair_first), by_heading(pair_second), by_heading(pair_valid), forward, inverse)])
    return out[None, None]


def solution(mesh):
    forward, inverse = make_tables(512)
    spec4 = P("wide", "narrow", None, None)
    spec5 = P("wide", "narrow", None, None, None)

    def run(traces, pair_first, pair_second, pair_valid):
        return local(
            jnp.asarray(forward), jnp.asarray(inverse), traces, pair_first, pair_second, pair_valid
        )

    return jax.shard_map(
        run, mesh=mesh, in_specs=(spec5, spec4, spec4, spec4), out_specs=spec5, check_vma=False
    )
```

```python
import functools
import math

import jax
import jax.numpy as jnp
import ml_dtypes
import numpy as np
from jax import lax
from jax.experimental import pallas as pl
from jax.experimental.pallas import tpu as pltpu
from jax.sharding import PartitionSpec as P

LAGS = 256
NFFT = 768
BLOCKS = 3
BINS = 128
CHUNK = 2
LAG = 2
CODE_MAX = 32767.0
MESH = pl.DeviceIdType.MESH
F32 = jnp.float32
BF16 = jnp.bfloat16


def split_np(table):
    high = table.astype(ml_dtypes.bfloat16)
    low = (table - high.astype(np.float64)).astype(ml_dtypes.bfloat16)
    return np.stack([high, low])


def make_tables(samples):
    freq = np.arange(NFFT // 2, dtype=np.float64) + 0.5
    step = 2.0 * math.pi / NFFT
    phase = np.arange(samples, dtype=np.float64)[:, None] * freq[None, :] * step
    parts = []
    for b in range(BLOCKS):
        cols = slice(b * BINS, (b + 1) * BINS)
        parts += [np.cos(phase[:, cols]), -np.sin(phase[:, cols])]
    forward = np.concatenate(parts, axis=1)
    lag = np.arange(LAGS, dtype=np.float64) - LAGS // 2
    phase = freq[:, None] * lag[None, :] * step
    scale = 2.0 / (NFFT * math.sqrt(samples))
    parts = []
    for b in range(BLOCKS):
        rows = slice(b * BINS, (b + 1) * BINS)
        parts += [np.cos(phase[rows]) * scale, -np.sin(phase[rows]) * scale]
    return split_np(forward), split_np(np.concatenate(parts, axis=0))


def split(v):
    high = v.astype(BF16)
    return high, (v - high.astype(F32)).astype(BF16)


def dot(a, b):
    return jnp.dot(a, b, preferred_element_type=F32)


def kernel(
    traces, first, second, valid, fwd_hbm, inv_hbm, out,
    raw, wide32, cells, part_own, sent_up, sent_down, got_up, got_down,
    weights, codes, fwd, inv, held,
    load_sem, table_sem, code_send, code_recv,
    x_send_left, x_send_right, x_from_left, x_from_right,
    y_send_up, y_send_down, y_from_up, y_from_down,
):
    events, channels, samples = traces.shape
    lanes = samples // 128
    chunks = channels // CHUNK
    rows, cols = lax.axis_size("wide"), lax.axis_size("narrow")
    row, col = lax.axis_index("wide"), lax.axis_index("narrow")
    left = {"narrow": lax.rem(col + cols - 1, cols)}
    right = {"narrow": lax.rem(col + 1, cols)}
    up = {"wide": lax.rem(row + rows - 1, rows)}
    down = {"wide": lax.rem(row + 1, rows)}
    has_left, has_right = col > 0, col < cols - 1
    has_up, has_down = row > 0, row < rows - 1
    sides = ((has_left, left), (has_right, right), (has_up, up), (has_down, down))

    load = pltpu.make_async_copy(traces, raw, load_sem)
    load.start()
    barrier = pltpu.get_barrier_semaphore()
    for has, peer in sides:
        @pl.when(has)
        def _():
            pl.semaphore_signal(barrier, inc=1, device_id=peer, device_id_type=MESH)

    load_fwd = pltpu.make_async_copy(fwd_hbm, fwd, table_sem.at[0])
    load_inv = pltpu.make_async_copy(inv_hbm, inv, table_sem.at[1])
    load_fwd.start()
    load_inv.start()

    slots = first.shape[2]
    codes[0, 0:9, 0:slots] = jnp.where(
        valid[:, 0, :] == 1, first[:, 0, :] * events + second[:, 0, :], -1
    )

    def blank(has, slot, block, first_row, row_count):
        @pl.when(jnp.logical_not(has))
        def _():
            codes[slot] = jnp.full(codes.shape[1:], -1, jnp.int32)

            def clear(n, _):
                block[n, first_row : first_row + row_count, :] = jnp.zeros(
                    (row_count, samples), block.dtype
                )
                return 0

            lax.fori_loop(0, block.shape[0], clear, 0)

    blank(has_left, 1, cells, 0, events)
    blank(has_right, 2, cells, 2 * events, events)
    blank(has_up, 3, got_up, 0, got_up.shape[1])
    blank(has_down, 4, got_down, 0, got_down.shape[1])

    def turn(group):
        for i in range(lanes):
            spread = raw[:, group * 8 : (group + 1) * 8, i * 128 : (i + 1) * 128].astype(F32)
            wide32[group, i] = spread.reshape(events * 8, 128)
        for n in range(8):
            for i in range(lanes):
                lane_block = wide32[group, i, pl.ds(n, events, stride=8), :]
                cells[group * 8 + n, events : 2 * events, i * 128 : (i + 1) * 128] = (
                    lane_block.astype(BF16)
                )

    def remote(src, dst, send, recv, peer):
        return pltpu.make_async_remote_copy(
            src_ref=src, dst_ref=dst, send_sem=send, recv_sem=recv,
            device_id=peer, device_id_type=MESH,
        )

    code_copies = [
        remote(codes.at[0], codes.at[slot], code_send.at[slot - 1], code_recv.at[slot - 1], peer)
        for slot, peer in ((2, left), (1, right), (4, up), (3, down))
    ]
    has_from = {1: has_left, 2: has_right, 3: has_up, 4: has_down}

    def x_left(k):
        block = pl.ds(k * CHUNK, CHUNK)
        return remote(
            cells.at[block, events : 2 * events, :], cells.at[block, 2 * events : 3 * events, :],
            x_send_left.at[k], x_from_right.at[k], left,
        )

    def x_right(k):
        block = pl.ds(k * CHUNK, CHUNK)
        return remote(
            cells.at[block, events : 2 * events, :], cells.at[block, 0:events, :],
            x_send_right.at[k], x_from_left.at[k], right,
        )

    def y_up(k):
        return remote(sent_up.at[k], got_down.at[k], y_send_up.at[k], y_from_down.at[k], up)

    def y_down(k):
        return remote(sent_down.at[k], got_up.at[k], y_send_down.at[k], y_from_up.at[k], down)

    def start_if(has, make):
        @pl.when(has)
        def _():
            make().start()

    def wait_send_if(has, make):
        @pl.when(has)
        def _():
            make().wait_send()

    def wait_recv_if(has, make):
        @pl.when(has)
        def _():
            make().wait_recv()

    def send_x(k):
        start_if(has_left, lambda: x_left(k))
        start_if(has_right, lambda: x_right(k))

    load.wait()
    turn(0)
    peers = sum(has.astype(jnp.int32) for has, _ in sides)
    pl.semaphore_wait(barrier, peers)
    for copy, (has, _) in zip(code_copies, sides):
        start_if(has, lambda: copy)
    for k in range(8 // CHUNK):
        send_x(k)
    for group in range(1, channels // 8):
        turn(group)

    for copy, slot, (has, _) in zip(code_copies, (2, 1, 4, 3), sides):
        wait_send_if(has, lambda: copy)
        wait_recv_if(has_from[slot], lambda: copy)

    ids = lax.broadcasted_iota(jnp.int32, (events, slots), 0)

    def ends(slot, heading):
        code = codes[slot, heading : heading + 1, 0:slots]
        live = code >= 0
        head = jnp.where(live, code // events, -1)
        tail = jnp.where(live, code % events, -1)
        return (
            jnp.where(ids == head, 1.0, 0.0).astype(BF16),
            jnp.where(ids == tail, 1.0, 0.0).astype(BF16),
        )

    def outer(a, b):
        return lax.dot_general(
            a, b, (((1,), (1,)), ((), ())), preferred_element_type=F32
        )

    for i in (-1, 0, 1):
        target = {-1: 3, 0: 0, 1: 4}[i]
        for j in (-1, 0, 1):
            source = {-1: 1, 0: 0, 1: 2}[j]
            head, tail = ends(target, (1 - i) * 3 + (j + 1))
            count = outer(head, tail)
            head, tail = ends(source, (i + 1) * 3 + (1 - j))
            count = count + outer(tail, head)
            weights[
                (i + 1) * events : (i + 2) * events, (j + 1) * events : (j + 2) * events
            ] = count.astype(BF16)

    load_fwd.wait()
    load_inv.wait()

    size = CHUNK * events
    diagonal = lax.broadcasted_iota(jnp.int32, (size, size), 0) == lax.broadcasted_iota(
        jnp.int32, (size, size), 1
    )

    def encode(ref, k, part):
        peak = jnp.max(jnp.abs(part), axis=1, keepdims=True)
        power = jnp.ceil(jnp.log2(jnp.maximum(peak, 1e-30)) + 1e-4)
        code = jnp.round(part * (jnp.exp2(-power) * CODE_MAX))
        ref[k, 0:size, :] = code.astype(jnp.int32).astype(jnp.int16)
        band = jnp.sum(jnp.where(diagonal, power, 0.0), axis=0, keepdims=True)
        ref[k, size : size + 16, 0:size] = (
            jnp.broadcast_to(band, (16, size)).astype(jnp.int32).astype(jnp.int16)
        )

    def decode(ref, k):
        band = ref[k, size : size + 16, 0:size].astype(jnp.int32).astype(F32)[0:1]
        power = jnp.sum(jnp.where(diagonal, band, 0.0), axis=1, keepdims=True)
        code = ref[k, 0:size, :].astype(jnp.int32).astype(F32)
        return code * (jnp.exp2(power) * (1.0 / CODE_MAX))

    def gather(k):
        @pl.when(k + 8 // CHUNK < chunks)
        def _():
            send_x(k + 8 // CHUNK)

        wait_recv_if(has_left, lambda: x_right(k))
        wait_recv_if(has_right, lambda: x_left(k))

        parts = [dot(weights[...], cells[k * CHUNK + n]) for n in range(CHUNK)]
        for n in range(CHUNK):
            part_own[k * CHUNK + n] = parts[n][events : 2 * events]
        encode(sent_up, k, jnp.concatenate([p[0:events] for p in parts], axis=0))
        encode(sent_down, k, jnp.concatenate([p[2 * events :] for p in parts], axis=0))
        start_if(has_up, lambda: y_up(k))
        start_if(has_down, lambda: y_down(k))

    def correlate(k):
        wait_recv_if(has_up, lambda: y_down(k))
        wait_recv_if(has_down, lambda: y_up(k))
        block = pl.ds(k * CHUNK, CHUNK)
        x = cells[block, events : 2 * events, :].reshape(size, samples)
        y = part_own[block].reshape(size, samples) + decode(got_up, k) + decode(got_down, k)
        y_high, y_low = split(y)
        stack3 = jnp.concatenate([x, y_high, y_low], axis=0)
        stack2 = jnp.concatenate([x, y_high], axis=0)
        total = jnp.zeros((size, LAGS), F32)
        for b in range(BLOCKS):
            span = slice(b * 2 * BINS, (b + 1) * 2 * BINS)
            coarse = dot(stack3, fwd[0, :, span])
            fine = dot(stack2, fwd[1, :, span])
            xs = coarse[0:size] + fine[0:size]
            ys = coarse[size : 2 * size] + coarse[2 * size :] + fine[size:]
            xr, xi = xs[:, :BINS], xs[:, BINS:]
            yr, yi = ys[:, :BINS], ys[:, BINS:]
            s = jnp.concatenate([xr * yr + xi * yi, xr * yi - xi * yr], axis=1)
            s_high, s_low = split(s)
            both = dot(jnp.concatenate([s_high, s_low], axis=0), inv[0, span, :])
            total = total + (both[:size] + both[size:] + dot(s_high, inv[1, span, :]))
        per_group = 8 // CHUNK
        for n in range(CHUNK):
            for i in range(LAGS // 128):
                held[i, pl.ds(k % per_group * CHUNK + n, events, stride=8), :] = total[
                    n * events : (n + 1) * events, i * 128 : (i + 1) * 128
                ]

        @pl.when(k % per_group == per_group - 1)
        def _():
            place = pl.ds(pl.multiple_of(k // per_group * 8, 8), 8)
            for i in range(LAGS // 128):
                out[:, place, i * 128 : (i + 1) * 128] = held[i].reshape(events, 8, 128)

    def step(k, _):
        @pl.when(k < chunks)
        def _():
            gather(k)

        @pl.when(k >= LAG)
        def _():
            correlate(k - LAG)

        return 0

    lax.fori_loop(0, chunks + LAG, step, 0)
    def finish(k, _):
        wait_send_if(has_left, lambda: x_left(k))
        wait_send_if(has_right, lambda: x_right(k))
        wait_send_if(has_up, lambda: y_up(k))
        wait_send_if(has_down, lambda: y_down(k))
        return 0

    lax.fori_loop(0, chunks, finish, 0)


def by_heading(pairs):
    return pairs.transpose(0, 2, 1, 3)[0]


def local(forward, inverse, traces, pair_first, pair_second, pair_valid):
    _, _, events, channels, samples = traces.shape
    chunks = channels // CHUNK
    part = pltpu.VMEM((channels, events, samples), F32)
    code = pltpu.VMEM((chunks, CHUNK * events + 16, samples), jnp.int16)
    in_hbm = pl.BlockSpec(memory_space=pltpu.HBM)
    in_vmem = pl.BlockSpec(memory_space=pltpu.VMEM)
    dma = pltpu.SemaphoreType.DMA
    out = pl.pallas_call(
        kernel,
        out_shape=jax.ShapeDtypeStruct((events, channels, LAGS), F32),
        in_specs=[in_hbm, in_vmem, in_vmem, in_vmem, in_hbm, in_hbm],
        out_specs=in_vmem,
        scratch_shapes=[
            pltpu.VMEM((events, channels, samples), BF16),
            pltpu.VMEM((channels // 8, samples // 128, events * 8, 128), F32),
            pltpu.VMEM((channels, 3 * events, samples), BF16),
            part, code, code, code, code,
            pltpu.VMEM((3 * events, 3 * events), BF16),
            pltpu.VMEM((5, 16, 128), jnp.int32),
            pltpu.VMEM(forward.shape, BF16),
            pltpu.VMEM(inverse.shape, BF16),
            pltpu.VMEM((LAGS // 128, events * 8, 128), F32),
            dma, dma((2,)), dma((4,)), dma((4,)),
        ] + [dma((chunks,))] * 8,
        compiler_params=pltpu.CompilerParams(
            collective_id=0, has_side_effects=True, vmem_limit_bytes=40 * 1024 * 1024
        ),
        cost_estimate=pl.CostEstimate(
            flops=8 * 10**9, bytes_accessed=6 * 10**6, transcendentals=0
        ),
        name="event_correlation",
    )(*[pltpu.with_memory_space_constraint(v, pltpu.HBM) for v in (traces[0, 0], by_heading(pair_first), by_heading(pair_second), by_heading(pair_valid), forward, inverse)])
    return out[None, None]


def solution(mesh):
    forward, inverse = make_tables(512)
    spec4 = P("wide", "narrow", None, None)
    spec5 = P("wide", "narrow", None, None, None)

    def run(traces, pair_first, pair_second, pair_valid):
        return local(
            jnp.asarray(forward), jnp.asarray(inverse), traces, pair_first, pair_second, pair_valid
        )

    return jax.shard_map(
        run, mesh=mesh, in_specs=(spec5, spec4, spec4, spec4), out_specs=spec5, check_vma=False
    )
```

```python
import functools
import math

import jax
import jax.numpy as jnp
import ml_dtypes
import numpy as np
from jax import lax
from jax.experimental import pallas as pl
from jax.experimental.pallas import tpu as pltpu
from jax.sharding import PartitionSpec as P

LAGS = 256
NFFT = 768
BLOCKS = 3
BINS = 128
CHUNK = 2
LAG = 2
SETTLE = 5
EARLY = 8
AHEAD = 4
CODE_MAX = 32767.0
MESH = pl.DeviceIdType.MESH
F32 = jnp.float32
BF16 = jnp.bfloat16


def split_np(table):
    high = table.astype(ml_dtypes.bfloat16)
    low = (table - high.astype(np.float64)).astype(ml_dtypes.bfloat16)
    return np.stack([high, low])


def make_tables(samples):
    freq = np.arange(NFFT // 2, dtype=np.float64) + 0.5
    step = 2.0 * math.pi / NFFT
    phase = np.arange(samples, dtype=np.float64)[:, None] * freq[None, :] * step
    parts = []
    for b in range(BLOCKS):
        cols = slice(b * BINS, (b + 1) * BINS)
        parts += [np.cos(phase[:, cols]), -np.sin(phase[:, cols])]
    forward = np.concatenate(parts, axis=1)
    lag = np.arange(LAGS, dtype=np.float64) - LAGS // 2
    phase = freq[:, None] * lag[None, :] * step
    scale = 2.0 / (NFFT * math.sqrt(samples))
    parts = []
    for b in range(BLOCKS):
        rows = slice(b * BINS, (b + 1) * BINS)
        parts += [np.cos(phase[rows]) * scale, -np.sin(phase[rows]) * scale]
    return split_np(forward), split_np(np.concatenate(parts, axis=0))


def split(v):
    high = v.astype(BF16)
    return high, (v - high.astype(F32)).astype(BF16)


def dot(a, b):
    return jnp.dot(a, b, preferred_element_type=F32)


def kernel(
    traces, first, second, valid, fwd_hbm, inv_hbm, out,
    raw, wide32, cells, part_own, sent_low, sent_high, got_low, got_high,
    weights, codes, fwd, inv, held,
    load_sem, table_sem, code_send, code_recv,
    x_send_low, x_send_high, x_from_low, x_from_high,
    y_send_low, y_send_high, y_from_low, y_from_high,
):
    events, channels, samples = traces.shape
    lanes = samples // 128
    chunks = channels // CHUNK
    rows, cols = lax.axis_size("wide"), lax.axis_size("narrow")
    row, col = lax.axis_index("wide"), lax.axis_index("narrow")
    left = {"narrow": lax.rem(col + cols - 1, cols)}
    right = {"narrow": lax.rem(col + 1, cols)}
    up = {"wide": lax.rem(row + rows - 1, rows)}
    down = {"wide": lax.rem(row + 1, rows)}
    has_left, has_right = col > 0, col < cols - 1
    has_up, has_down = row > 0, row < rows - 1
    sides = ((has_left, left), (has_right, right), (has_up, up), (has_down, down))

    load = pltpu.make_async_copy(traces, raw, load_sem)
    load.start()
    barrier = pltpu.get_barrier_semaphore()
    for has, peer in sides:
        @pl.when(has)
        def _():
            pl.semaphore_signal(barrier, inc=1, device_id=peer, device_id_type=MESH)

    load_fwd = pltpu.make_async_copy(fwd_hbm, fwd, table_sem.at[0])
    load_inv = pltpu.make_async_copy(inv_hbm, inv, table_sem.at[1])
    load_fwd.start()
    load_inv.start()

    slots = first.shape[2]
    codes[0, 0:9, 0:slots] = jnp.where(
        valid[:, 0, :] == 1, first[:, 0, :] * events + second[:, 0, :], -1
    )

    def blank(has, slot, block, span, first_row, row_count):
        @pl.when(jnp.logical_not(has))
        def _():
            codes[slot] = jnp.full(codes.shape[1:], -1, jnp.int32)

            def clear(n, _):
                block[n, first_row : first_row + row_count, :] = jnp.zeros(
                    (row_count, block.shape[2]), block.dtype
                )
                return 0

            lax.fori_loop(*span, clear, 0)

    split_at = EARLY * CHUNK
    early, late = (0, EARLY), (EARLY, chunks)
    blank(has_left, 1, cells, (0, split_at), 0, events)
    blank(has_right, 2, cells, (0, split_at), 2 * events, events)
    blank(has_up, 3, cells, (split_at, channels), 0, events)
    blank(has_down, 4, cells, (split_at, channels), 2 * events, events)
    blank(has_up, 3, got_low, early, 0, got_low.shape[1])
    blank(has_down, 4, got_high, early, 0, got_high.shape[1])
    blank(has_left, 1, got_low, late, 0, got_low.shape[1])
    blank(has_right, 2, got_high, late, 0, got_high.shape[1])

    def turn(group):
        for i in range(lanes):
            spread = raw[:, group * 8 : (group + 1) * 8, i * 128 : (i + 1) * 128].astype(F32)
            wide32[group, i] = spread.reshape(events * 8, 128)
        for n in range(8):
            for i in range(lanes):
                lane_block = wide32[group, i, pl.ds(n, events, stride=8), :]
                cells[group * 8 + n, events : 2 * events, i * 128 : (i + 1) * 128] = (
                    lane_block.astype(BF16)
                )

    def remote(src, dst, send, recv, peer):
        return pltpu.make_async_remote_copy(
            src_ref=src, dst_ref=dst, send_sem=send, recv_sem=recv,
            device_id=peer, device_id_type=MESH,
        )

    code_copies = [
        remote(codes.at[0], codes.at[slot], code_send.at[slot - 1], code_recv.at[slot - 1], peer)
        for slot, peer in ((2, left), (1, right), (4, up), (3, down))
    ]
    has_from = {1: has_left, 2: has_right, 3: has_up, 4: has_down}

    def traces_low(k, peer):
        block = pl.ds(k * CHUNK, CHUNK)
        return remote(
            cells.at[block, events : 2 * events, :], cells.at[block, 2 * events : 3 * events, :],
            x_send_low.at[k], x_from_high.at[k], peer,
        )

    def traces_high(k, peer):
        block = pl.ds(k * CHUNK, CHUNK)
        return remote(
            cells.at[block, events : 2 * events, :], cells.at[block, 0:events, :],
            x_send_high.at[k], x_from_low.at[k], peer,
        )

    def sums_low(k, peer):
        return remote(sent_low.at[k], got_high.at[k], y_send_low.at[k], y_from_high.at[k], peer)

    def sums_high(k, peer):
        return remote(sent_high.at[k], got_low.at[k], y_send_high.at[k], y_from_low.at[k], peer)

    across = ((has_left, left), (has_right, right))
    along = ((has_up, up), (has_down, down))

    def start(make_low, make_high, k, peers):
        (has_low, low), (has_high, high) = peers
        start_if(has_low, lambda: make_low(k, low))
        start_if(has_high, lambda: make_high(k, high))

    def wait_recv(make_low, make_high, k, peers):
        (has_low, low), (has_high, high) = peers
        wait_recv_if(has_low, lambda: make_high(k, high))
        wait_recv_if(has_high, lambda: make_low(k, low))

    def wait_send(make_low, make_high, k, peers):
        (has_low, low), (has_high, high) = peers
        wait_send_if(has_low, lambda: make_low(k, low))
        wait_send_if(has_high, lambda: make_high(k, high))

    def by_order(act, make_low, make_high, k, early_peers, late_peers):
        if isinstance(k, int):
            act(make_low, make_high, k, early_peers if k < EARLY else late_peers)
            return

        @pl.when(k < EARLY)
        def _():
            act(make_low, make_high, k, early_peers)

        @pl.when(k >= EARLY)
        def _():
            act(make_low, make_high, k, late_peers)

    def start_if(has, make):
        @pl.when(has)
        def _():
            make().start()

    def wait_send_if(has, make):
        @pl.when(has)
        def _():
            make().wait_send()

    def wait_recv_if(has, make):
        @pl.when(has)
        def _():
            make().wait_recv()

    def send_traces(k):
        by_order(start, traces_low, traces_high, k, across, along)

    load.wait()
    turn(0)
    peers = sum(has.astype(jnp.int32) for has, _ in sides)
    pl.semaphore_wait(barrier, peers)
    for copy, (has, _) in zip(code_copies, sides):
        start_if(has, lambda: copy)
    for k in range(AHEAD):
        send_traces(k)
    for group in range(channels // 8 - 1, 0, -1):
        turn(group)
        for k in range(group * 8 // CHUNK, (group + 1) * 8 // CHUNK):
            if k >= EARLY:
                send_traces(k)

    for copy, slot, (has, _) in zip(code_copies, (2, 1, 4, 3), sides):
        wait_send_if(has, lambda: copy)
        wait_recv_if(has_from[slot], lambda: copy)

    ids = lax.broadcasted_iota(jnp.int32, (events, slots), 0)

    def ends(slot, heading):
        code = codes[slot, heading : heading + 1, 0:slots]
        live = code >= 0
        head = jnp.where(live, code // events, -1)
        tail = jnp.where(live, code % events, -1)
        return (
            jnp.where(ids == head, 1.0, 0.0).astype(BF16),
            jnp.where(ids == tail, 1.0, 0.0).astype(BF16),
        )

    def outer(a, b):
        return lax.dot_general(
            a, b, (((1,), (1,)), ((), ())), preferred_element_type=F32
        )

    def count(target, target_heading, source, source_heading):
        head, tail = ends(target, target_heading)
        pairs = outer(head, tail)
        head, tail = ends(source, source_heading)
        return (pairs + outer(tail, head)).astype(BF16)

    by_row = {-1: 3, 0: 0, 1: 4}
    by_col = {-1: 1, 0: 0, 1: 2}
    for i in (-1, 0, 1):
        for j in (-1, 0, 1):
            rows_at = pl.ds((i + 1) * events, events)
            weights[0, rows_at, (j + 1) * events : (j + 2) * events] = count(
                by_row[i], (1 - i) * 3 + (j + 1), by_col[j], (i + 1) * 3 + (1 - j)
            )
            weights[1, rows_at, (j + 1) * events : (j + 2) * events] = count(
                by_col[i], (j + 1) * 3 + (1 - i), by_row[j], (1 - j) * 3 + (i + 1)
            )

    load_fwd.wait()
    load_inv.wait()

    size = CHUNK * events
    diagonal = lax.broadcasted_iota(jnp.int32, (size, size), 0) == lax.broadcasted_iota(
        jnp.int32, (size, size), 1
    )

    def encode(ref, k, part):
        peak = jnp.max(jnp.abs(part), axis=1, keepdims=True)
        power = jnp.ceil(jnp.log2(jnp.maximum(peak, 1e-30)) + 1e-4)
        code = jnp.round(part * (jnp.exp2(-power) * CODE_MAX))
        code = code.astype(jnp.int32).astype(jnp.int16)
        for i in range(lanes):
            ref[k, i * size : (i + 1) * size, :] = code[:, i * 128 : (i + 1) * 128]
        band = jnp.sum(jnp.where(diagonal, power, 0.0), axis=0, keepdims=True)
        ref[k, lanes * size : lanes * size + 16, 0:size] = (
            jnp.broadcast_to(band, (16, size)).astype(jnp.int32).astype(jnp.int16)
        )

    def decode(ref, k):
        band = ref[k, lanes * size : lanes * size + 16, 0:size].astype(jnp.int32).astype(F32)[0:1]
        power = jnp.sum(jnp.where(diagonal, band, 0.0), axis=1, keepdims=True)
        code = jnp.concatenate(
            [ref[k, i * size : (i + 1) * size, :] for i in range(lanes)], axis=1
        ).astype(jnp.int32).astype(F32)
        return code * (jnp.exp2(power) * (1.0 / CODE_MAX))

    def gather(k, late):
        wait_recv(traces_low, traces_high, k, along if late else across)
        parts = [dot(weights[int(late)], cells[k * CHUNK + n]) for n in range(CHUNK)]
        for n in range(CHUNK):
            part_own[k * CHUNK + n] = parts[n][events : 2 * events]
        encode(sent_low, k, jnp.concatenate([p[0:events] for p in parts], axis=0))
        encode(sent_high, k, jnp.concatenate([p[2 * events :] for p in parts], axis=0))
        start(sums_low, sums_high, k, across if late else along)

    def correlate(k):
        by_order(wait_recv, sums_low, sums_high, k, along, across)
        block = pl.ds(k * CHUNK, CHUNK)
        x = cells[block, events : 2 * events, :].reshape(size, samples)
        y = part_own[block].reshape(size, samples) + decode(got_low, k) + decode(got_high, k)
        y_high, y_low = split(y)
        stack3 = jnp.concatenate([x, y_high, y_low], axis=0)
        stack2 = jnp.concatenate([x, y_high], axis=0)
        total = jnp.zeros((size, LAGS), F32)
        for b in range(BLOCKS):
            span = slice(b * 2 * BINS, (b + 1) * 2 * BINS)
            coarse = dot(stack3, fwd[0, :, span])
            fine = dot(stack2, fwd[1, :, span])
            xs = coarse[0:size] + fine[0:size]
            ys = coarse[size : 2 * size] + coarse[2 * size :] + fine[size:]
            xr, xi = xs[:, :BINS], xs[:, BINS:]
            yr, yi = ys[:, :BINS], ys[:, BINS:]
            s = jnp.concatenate([xr * yr + xi * yi, xr * yi - xi * yr], axis=1)
            s_high, s_low = split(s)
            both = dot(jnp.concatenate([s_high, s_low], axis=0), inv[0, span, :])
            total = total + (both[:size] + both[size:] + dot(s_high, inv[1, span, :]))
        per_group = 8 // CHUNK
        for n in range(CHUNK):
            for i in range(LAGS // 128):
                held[i, pl.ds(k % per_group * CHUNK + n, events, stride=8), :] = total[
                    n * events : (n + 1) * events, i * 128 : (i + 1) * 128
                ]

        @pl.when(k % per_group == per_group - 1)
        def _():
            place = pl.ds(pl.multiple_of(k // per_group * 8, 8), 8)
            for i in range(LAGS // 128):
                out[:, place, i * 128 : (i + 1) * 128] = held[i].reshape(events, 8, 128)

    def finish(k):
        by_order(wait_send, traces_low, traces_high, k, across, along)
        by_order(wait_send, sums_low, sums_high, k, along, across)

    def step(k, _):
        @pl.when(k + AHEAD < EARLY)
        def _():
            send_traces(k + AHEAD)

        @pl.when(k < EARLY)
        def _():
            gather(k, False)

        @pl.when((k >= EARLY - AHEAD) & (k < chunks - AHEAD))
        def _():
            gather(k + AHEAD, True)

        @pl.when(k >= LAG)
        def _():
            correlate(k - LAG)

        @pl.when(k >= SETTLE)
        def _():
            finish(k - SETTLE)

        return 0

    lax.fori_loop(0, chunks + LAG, step, 0)

    for k in range(chunks + LAG - SETTLE, chunks):
        finish(k)


def by_heading(pairs):
    return pairs.transpose(0, 2, 1, 3)[0]


def local(forward, inverse, traces, pair_first, pair_second, pair_valid):
    _, _, events, channels, samples = traces.shape
    chunks = channels // CHUNK
    part = pltpu.VMEM((channels, events, samples), F32)
    code = pltpu.VMEM((chunks, CHUNK * events * samples // 128 + 16, 128), jnp.int16)
    in_hbm = pl.BlockSpec(memory_space=pltpu.HBM)
    in_vmem = pl.BlockSpec(memory_space=pltpu.VMEM)
    dma = pltpu.SemaphoreType.DMA
    out = pl.pallas_call(
        kernel,
        out_shape=jax.ShapeDtypeStruct((events, channels, LAGS), F32),
        in_specs=[in_hbm, in_vmem, in_vmem, in_vmem, in_hbm, in_hbm],
        out_specs=in_vmem,
        scratch_shapes=[
            pltpu.VMEM((events, channels, samples), BF16),
            pltpu.VMEM((channels // 8, samples // 128, events * 8, 128), F32),
            pltpu.VMEM((channels, 3 * events, samples), BF16),
            part, code, code, code, code,
            pltpu.VMEM((2, 3 * events, 3 * events), BF16),
            pltpu.VMEM((5, 16, 128), jnp.int32),
            pltpu.VMEM(forward.shape, BF16),
            pltpu.VMEM(inverse.shape, BF16),
            pltpu.VMEM((LAGS // 128, events * 8, 128), F32),
            dma, dma((2,)), dma((4,)), dma((4,)),
        ] + [dma((chunks,))] * 8,
        compiler_params=pltpu.CompilerParams(
            collective_id=0, has_side_effects=True, vmem_limit_bytes=40 * 1024 * 1024
        ),
        cost_estimate=pl.CostEstimate(
            flops=8 * 10**9, bytes_accessed=6 * 10**6, transcendentals=0
        ),
        name="event_correlation",
    )(*[pltpu.with_memory_space_constraint(v, pltpu.HBM) for v in (traces[0, 0], by_heading(pair_first), by_heading(pair_second), by_heading(pair_valid), forward, inverse)])
    return out[None, None]


def solution(mesh):
    forward, inverse = make_tables(512)
    spec4 = P("wide", "narrow", None, None)
    spec5 = P("wide", "narrow", None, None, None)

    def run(traces, pair_first, pair_second, pair_valid):
        return local(
            jnp.asarray(forward), jnp.asarray(inverse), traces, pair_first, pair_second, pair_valid
        )

    return jax.shard_map(
        run, mesh=mesh, in_specs=(spec5, spec4, spec4, spec4), out_specs=spec5, check_vma=False
    )
```

```python
import functools
import math

import jax
import jax.numpy as jnp
import ml_dtypes
import numpy as np
from jax import lax
from jax.experimental import pallas as pl
from jax.experimental.pallas import tpu as pltpu
from jax.sharding import PartitionSpec as P

LAGS = 256
BLOCK = 128
SHIFTS = (-1, 0, 1)
CHUNK = 2
LAG = 3
SETTLE = 6
HYBRID = 5
EARLY = 8
AHEAD = 4
CODE_MAX = 32767.0
MESH = pl.DeviceIdType.MESH
F32 = jnp.float32
BF16 = jnp.bfloat16


def split_np(table):
    high = table.astype(ml_dtypes.bfloat16)
    low = (table - high.astype(np.float64)).astype(ml_dtypes.bfloat16)
    return np.stack([high, low])


def make_tables(samples):
    freq = np.arange(BLOCK, dtype=np.float64) + 0.5
    step = 2.0 * math.pi / (2 * BLOCK)
    phase = np.arange(BLOCK, dtype=np.float64)[:, None] * freq[None, :] * step
    forward = split_np(np.concatenate([np.cos(phase), -np.sin(phase)], axis=1))
    lag = np.arange(LAGS, dtype=np.float64) - LAGS // 2
    scale = 1.0 / (BLOCK * math.sqrt(samples))
    parts = []
    for d in SHIFTS:
        offset = lag - BLOCK * d
        phase = freq[:, None] * offset[None, :] * step
        inside = (np.abs(offset) < BLOCK)[None, :] * scale
        parts += [np.cos(phase) * inside, -np.sin(phase) * inside]
    return np.concatenate(list(forward), axis=0), split_np(np.concatenate(parts, axis=0))


def split(v):
    high = v.astype(BF16)
    return high, (v - high.astype(F32)).astype(BF16)


def dot(a, b):
    return jnp.dot(a, b, preferred_element_type=F32)


def when(condition):
    if isinstance(condition, bool):
        return (lambda body: body()) if condition else (lambda body: None)
    return pl.when(condition)


def kernel(
    traces, first, second, valid, fwd_hbm, inv_hbm, out,
    raw, wide32, cells, part_own, sent_low, sent_high, got_low, got_high,
    side, back_out, back_in, tail_out, tail_in, acc,
    weights, codes, fwd, inv, held,
    load_sem, table_sem, code_send, code_recv,
    x_send_low, x_send_high, x_from_low, x_from_high,
    y_send_low, y_send_high, y_from_low, y_from_high,
    side_send, side_recv, back_send, back_recv, tail_send, tail_recv,
):
    events, channels, samples = traces.shape
    lanes = samples // 128
    chunks = channels // CHUNK
    last = chunks - 1
    rows, cols = lax.axis_size("wide"), lax.axis_size("narrow")
    row, col = lax.axis_index("wide"), lax.axis_index("narrow")
    left = {"narrow": lax.rem(col + cols - 1, cols)}
    right = {"narrow": lax.rem(col + 1, cols)}
    up = {"wide": lax.rem(row + rows - 1, rows)}
    down = {"wide": lax.rem(row + 1, rows)}
    has_left, has_right = col > 0, col < cols - 1
    has_up, has_down = row > 0, row < rows - 1
    sides = ((has_left, left), (has_right, right), (has_up, up), (has_down, down))

    load = pltpu.make_async_copy(traces, raw, load_sem)
    load.start()
    barrier = pltpu.get_barrier_semaphore()
    for has, peer in sides:
        @pl.when(has)
        def _():
            pl.semaphore_signal(barrier, inc=1, device_id=peer, device_id_type=MESH)

    slots = first.shape[2]
    codes[0, 0:9, 0:slots] = jnp.where(
        valid[:, 0, :] == 1, first[:, 0, :] * events + second[:, 0, :], -1
    )

    def spread(group):
        for i in range(lanes):
            part = raw[:, group * 8 : (group + 1) * 8, i * 128 : (i + 1) * 128].astype(F32)
            wide32[group, i] = part.reshape(events * 8, 128)

    def turn(k):
        if k * CHUNK % 8 == 0:
            spread(k * CHUNK // 8)
        for c in range(k * CHUNK, (k + 1) * CHUNK):
            for i in range(lanes):
                lane_block = wide32[c // 8, i, pl.ds(c % 8, events, stride=8), :]
                cells[c, events : 2 * events, i * 128 : (i + 1) * 128] = lane_block.astype(BF16)

    back_rows = back_in.shape[1] // 2

    def remote(src, dst, send, recv, peer):
        return pltpu.make_async_remote_copy(
            src_ref=src, dst_ref=dst, send_sem=send, recv_sem=recv,
            device_id=peer, device_id_type=MESH,
        )

    code_copies = [
        remote(codes.at[0], codes.at[slot], code_send.at[slot - 1], code_recv.at[slot - 1], peer)
        for slot, peer in ((2, left), (1, right), (4, up), (3, down))
    ]
    has_from = {1: has_left, 2: has_right, 3: has_up, 4: has_down}

    def traces_low(k, peer):
        block = pl.ds(k * CHUNK, CHUNK)
        return remote(
            cells.at[block, events : 2 * events, :], cells.at[block, 2 * events : 3 * events, :],
            x_send_low.at[k], x_from_high.at[k], peer,
        )

    def traces_high(k, peer):
        block = pl.ds(k * CHUNK, CHUNK)
        return remote(
            cells.at[block, events : 2 * events, :], cells.at[block, 0:events, :],
            x_send_high.at[k], x_from_low.at[k], peer,
        )

    def sums_low(k, peer):
        return remote(sent_low.at[k], got_high.at[k], y_send_low.at[k], y_from_high.at[k], peer)

    def sums_high(k, peer):
        return remote(sent_high.at[k], got_low.at[k], y_send_high.at[k], y_from_low.at[k], peer)

    across = ((has_left, left), (has_right, right))
    along = ((has_up, up), (has_down, down))

    def start(make_low, make_high, k, peers):
        (has_low, low), (has_high, high) = peers
        start_if(has_low, lambda: make_low(k, low))
        start_if(has_high, lambda: make_high(k, high))

    def wait_recv(make_low, make_high, k, peers):
        (has_low, low), (has_high, high) = peers
        wait_recv_if(has_low, lambda: make_high(k, high))
        wait_recv_if(has_high, lambda: make_low(k, low))

    def wait_send(make_low, make_high, k, peers):
        (has_low, low), (has_high, high) = peers
        wait_send_if(has_low, lambda: make_low(k, low))
        wait_send_if(has_high, lambda: make_high(k, high))

    def by_axis(act, make_low, make_high, k, is_across):
        @when(is_across)
        def _():
            act(make_low, make_high, k, across)

        @when(not is_across if isinstance(is_across, bool) else jnp.logical_not(is_across))
        def _():
            act(make_low, make_high, k, along)

    def on_traces(act, k):
        by_axis(act, traces_low, traces_high, k, (k >= HYBRID) & (k < EARLY))

    def on_sums(act, k):
        by_axis(act, sums_low, sums_high, k, k >= EARLY)

    def side_copy(k, n):
        return remote(
            cells.at[k * CHUNK + n, events : 2 * events, :],
            side.at[k, n * events : (n + 1) * events, :],
            side_send.at[k, n], side_recv.at[k, n], (right, left)[n],
        )

    def back_copy(k, n):
        span = slice(n * back_rows, (n + 1) * back_rows)
        return remote(
            back_out.at[k, span, :], back_in.at[k, span, :],
            back_send.at[k, n], back_recv.at[k, n], (left, right)[n],
        )

    has_target, has_origin = (has_right, has_left), (has_left, has_right)

    def start_if(has, make):
        @pl.when(has)
        def _():
            make().start()

    def wait_send_if(has, make):
        @pl.when(has)
        def _():
            make().wait_send()

    def wait_recv_if(has, make):
        @pl.when(has)
        def _():
            make().wait_recv()

    load.wait()
    load_fwd = pltpu.make_async_copy(fwd_hbm, fwd, table_sem.at[0])
    load_inv = pltpu.make_async_copy(inv_hbm, inv, table_sem.at[1])
    load_fwd.start()
    load_inv.start()

    turn(0)
    peers = sum(has.astype(jnp.int32) for has, _ in sides)
    pl.semaphore_wait(barrier, peers)
    for k in range(HYBRID):
        if k > 0:
            turn(k)
        for n in range(CHUNK):
            start_if(has_target[n], lambda: side_copy(k, n))
        if k == 0:
            for copy, (has, _) in zip(code_copies, sides):
                start_if(has, lambda: copy)
        on_traces(start, k)
    for k in range(HYBRID, chunks):
        turn(k)

    def blank(has, slot, block, span, first_row, row_count):
        @pl.when(jnp.logical_not(has))
        def _():
            codes[slot] = jnp.full(codes.shape[1:], -1, jnp.int32)

            def clear(n, _):
                block[n, first_row : first_row + row_count, :] = jnp.zeros(
                    (row_count, block.shape[2]), block.dtype
                )
                return 0

            lax.fori_loop(*span, clear, 0)

    hybrid_to, early_to = HYBRID * CHUNK, EARLY * CHUNK
    for span in ((0, hybrid_to), (early_to, channels)):
        blank(has_up, 3, cells, span, 0, events)
        blank(has_down, 4, cells, span, 2 * events, events)
    blank(has_left, 1, cells, (hybrid_to, early_to), 0, events)
    blank(has_right, 2, cells, (hybrid_to, early_to), 2 * events, events)
    blank(has_up, 3, got_low, (0, EARLY), 0, got_low.shape[1])
    blank(has_down, 4, got_high, (0, EARLY), 0, got_high.shape[1])
    blank(has_left, 1, got_low, (EARLY, last), 0, got_low.shape[1])
    blank(has_right, 2, got_high, (EARLY, last), 0, got_high.shape[1])
    blank(has_left, 1, tail_in.at[0], (0, CHUNK), 0, tail_in.shape[2])
    blank(has_right, 2, tail_in.at[1], (0, CHUNK), 0, tail_in.shape[2])
    blank(has_left, 1, side, (0, HYBRID), 0, events)
    blank(has_right, 2, side, (0, HYBRID), events, events)
    blank(has_right, 2, back_in, (0, HYBRID), 0, back_rows)
    blank(has_left, 1, back_in, (0, HYBRID), back_rows, back_rows)

    for copy, slot, (has, _) in zip(code_copies, (2, 1, 4, 3), sides):
        wait_send_if(has, lambda: copy)
        wait_recv_if(has_from[slot], lambda: copy)

    ids = lax.broadcasted_iota(jnp.int32, (events, slots), 0)

    def ends(slot, heading):
        code = codes[slot, heading : heading + 1, 0:slots]
        live = code >= 0
        head = jnp.where(live, code // events, -1)
        tail = jnp.where(live, code % events, -1)
        return (
            jnp.where(ids == head, 1.0, 0.0).astype(BF16),
            jnp.where(ids == tail, 1.0, 0.0).astype(BF16),
        )

    def outer(a, b):
        return lax.dot_general(
            a, b, (((1,), (1,)), ((), ())), preferred_element_type=F32
        )

    def count(target, target_heading, source, source_heading):
        head, tail = ends(target, target_heading)
        pairs = outer(head, tail)
        head, tail = ends(source, source_heading)
        return (pairs + outer(tail, head)).astype(BF16)

    by_row = {-1: 3, 0: 0, 1: 4}
    by_col = {-1: 1, 0: 0, 1: 2}
    for i in (-1, 0, 1):
        for j in (-1, 0, 1):
            rows_at = pl.ds((i + 1) * events, events)
            weights[0, rows_at, (j + 1) * events : (j + 2) * events] = count(
                by_row[i], (1 - i) * 3 + (j + 1), by_col[j], (i + 1) * 3 + (1 - j)
            )
            weights[1, rows_at, (j + 1) * events : (j + 2) * events] = count(
                by_col[i], (j + 1) * 3 + (1 - i), by_row[j], (1 - j) * 3 + (i + 1)
            )

    load_fwd.wait()
    load_inv.wait()

    size = CHUNK * events

    def diagonal(n):
        at = [lax.broadcasted_iota(jnp.int32, (n, n), dim) for dim in (0, 1)]
        return at[0] == at[1]

    def encoded(part):
        n = part.shape[0]
        peak = jnp.max(jnp.abs(part), axis=1, keepdims=True)
        power = jnp.ceil(jnp.log2(jnp.maximum(peak, 1e-30)) + 1e-4)
        code = jnp.round(part * (jnp.exp2(-power) * CODE_MAX))
        band = jnp.sum(jnp.where(diagonal(n), power, 0.0), axis=0, keepdims=True)
        band = jnp.broadcast_to(band, (16, n)).astype(jnp.int32).astype(jnp.int16)
        return code.astype(jnp.int32).astype(jnp.int16), band

    def encode(ref, at, part):
        n = part.shape[0]
        code, band = encoded(part)
        for i in range(lanes):
            ref[*at, i * n : (i + 1) * n, :] = code[:, i * 128 : (i + 1) * 128]
        ref[*at, lanes * n : lanes * n + 16, 0:n] = band

    def decode(ref, at, n):
        band = ref[*at, lanes * n : lanes * n + 16, 0:n].astype(jnp.int32).astype(F32)[0:1]
        power = jnp.sum(jnp.where(diagonal(n), band, 0.0), axis=1, keepdims=True)
        code = jnp.concatenate(
            [ref[*at, i * n : (i + 1) * n, :] for i in range(lanes)], axis=1
        ).astype(jnp.int32).astype(F32)
        return code * (jnp.exp2(power) * (1.0 / CODE_MAX))

    def gather(k, late):
        wait_recv(traces_low, traces_high, k, along if late else across)
        parts = [dot(weights[int(late)], cells[k * CHUNK + n]) for n in range(CHUNK)]
        for n in range(CHUNK):
            part_own[k * CHUNK + n] = parts[n][events : 2 * events]
        encode(sent_low, (k,), jnp.concatenate([p[0:events] for p in parts], axis=0))
        encode(sent_high, (k,), jnp.concatenate([p[2 * events :] for p in parts], axis=0))
        start(sums_low, sums_high, k, across if late else along)

    def correlation(x, y):
        size = x.shape[0]
        y_high, y_low = split(y)
        stack = []
        for v in (x, y_high, y_low):
            for i in range(lanes):
                block = v[:, i * BLOCK : (i + 1) * BLOCK]
                stack.append(jnp.concatenate([block, block], axis=1))
        spectra = dot(jnp.concatenate(stack, axis=0), fwd[...])
        spectra = [spectra[n * size : (n + 1) * size] for n in range(3 * lanes)]
        xs = spectra[:lanes]
        ys = [spectra[lanes + i] + spectra[2 * lanes + i] for i in range(lanes)]
        total = jnp.zeros((size, LAGS), F32)
        for n, d in enumerate(SHIFTS):
            real, imag = 0.0, 0.0
            for i in range(max(0, -d), min(lanes, lanes - d)):
                xr, xi = xs[i][:, :BLOCK], xs[i][:, BLOCK:]
                yr, yi = ys[i + d][:, :BLOCK], ys[i + d][:, BLOCK:]
                real = real + (xr * yr + xi * yi)
                imag = imag + (xr * yi - xi * yr)
            s_high, s_low = split(jnp.concatenate([real, imag], axis=1))
            span = slice(n * 2 * BLOCK, (n + 1) * 2 * BLOCK)
            both = dot(jnp.concatenate([s_high, s_low], axis=0), inv[0, span, :])
            total = total + (both[:size] + both[size:] + dot(s_high, inv[1, span, :]))
        return total

    def hybrid_gather(k):
        on_traces(wait_recv, k)
        for n in range(CHUNK):
            wait_recv_if(has_origin[n], lambda: side_copy(k, n))
        c = k * CHUNK
        column_first = dot(weights[1, 0 : 2 * events, :], cells[c])
        column_second = dot(weights[1, events : 3 * events, :], cells[c + 1])
        side_first = dot(weights[0, :, 0:events], side[k, 0:events, :])
        side_second = dot(weights[0, :, 2 * events : 3 * events], side[k, events : 2 * events, :])
        part_own[c] = column_first[events:] + side_first[events : 2 * events]
        part_own[c + 1] = column_second[0:events] + side_second[events : 2 * events]
        encode(sent_low, (k,), jnp.concatenate([side_first[0:events], side_second[0:events]], axis=0))
        encode(
            sent_high, (k,),
            jnp.concatenate([side_first[2 * events :], side_second[2 * events :]], axis=0),
        )
        on_sums(start, k)
        returned = jnp.concatenate([column_first[0:events], column_second[events:]], axis=0)
        code, band = encoded(correlation(side[k], returned))
        for n in range(CHUNK):
            base = n * back_rows
            for i in range(LAGS // 128):
                back_out[k, base + i * events : base + (i + 1) * events, :] = code[
                    n * events : (n + 1) * events, i * 128 : (i + 1) * 128
                ]
            back_out[k, base + back_rows - 16 : base + back_rows, :] = band
            start_if(has_origin[n], lambda: back_copy(k, n))

    def add_back(k):
        for n in range(CHUNK):
            wait_recv_if(has_target[n], lambda: back_copy(k, n))
        bands = [
            back_in[k, (n + 1) * back_rows - 16 : (n + 1) * back_rows, :].astype(jnp.int32)
            for n in range(CHUNK)
        ]
        lane = lax.broadcasted_iota(jnp.int32, (16, size), 1)
        band = jnp.where(lane < events, bands[0], bands[1]).astype(F32)[0:1]
        power = jnp.sum(jnp.where(diagonal(size), band, 0.0), axis=1, keepdims=True)
        code = jnp.concatenate(
            [
                jnp.concatenate(
                    [
                        back_in[k, n * back_rows + i * events : n * back_rows + (i + 1) * events, :]
                        for i in range(LAGS // 128)
                    ],
                    axis=1,
                )
                for n in range(CHUNK)
            ],
            axis=0,
        )
        acc[...] += code.astype(jnp.int32).astype(F32) * (jnp.exp2(power) * (1.0 / CODE_MAX))

    def tail_low(n):
        return remote(
            tail_out.at[0, n], tail_in.at[1, n], tail_send.at[0, n], tail_recv.at[1, n], left
        )

    def tail_high(n):
        return remote(
            tail_out.at[1, n], tail_in.at[0, n], tail_send.at[1, n], tail_recv.at[0, n], right
        )

    def gather_last():
        wait_recv(traces_low, traces_high, last, along)
        for n in range(CHUNK):
            c = last * CHUNK + n
            part = dot(weights[1], cells[c])
            part_own[c] = part[events : 2 * events]
            encode(tail_out, (0, n), part[0:events])
            encode(tail_out, (1, n), part[2 * events :])
            start_if(has_left, lambda: tail_low(n))
            start_if(has_right, lambda: tail_high(n))

    def correlate_last():
        for n in range(CHUNK):
            c = last * CHUNK + n
            wait_recv_if(has_left, lambda: tail_high(n))
            wait_recv_if(has_right, lambda: tail_low(n))
            y = part_own[c] + decode(tail_in, (0, n), events) + decode(tail_in, (1, n), events)
            keep(c, correlation(cells[c, events : 2 * events, :], y))

    def keep(c, rows):
        for i in range(LAGS // 128):
            held[i, pl.ds(c % 8, events, stride=8), :] = rows[:, i * 128 : (i + 1) * 128]

    def flush(group):
        place = pl.ds(group * 8, 8)
        if not isinstance(group, int):
            place = pl.ds(pl.multiple_of(group * 8, 8), 8)
        for i in range(LAGS // 128):
            out[:, place, i * 128 : (i + 1) * 128] = held[i].reshape(events, 8, 128)

    def correlate(k):
        on_sums(wait_recv, k)
        block = pl.ds(k * CHUNK, CHUNK)
        x = cells[block, events : 2 * events, :].reshape(size, samples)
        y = part_own[block].reshape(size, samples) + decode(got_low, (k,), size) + decode(got_high, (k,), size)
        acc[...] = correlation(x, y)

        @pl.when(k < HYBRID)
        def _():
            add_back(k)

        total = acc[...]
        per_group = 8 // CHUNK
        for n in range(CHUNK):
            keep(k * CHUNK + n, total[n * events : (n + 1) * events])

        @pl.when(k % per_group == per_group - 1)
        def _():
            flush(k // per_group)

    def finish(k):
        on_traces(wait_send, k)

        @when(k < last)
        def _():
            on_sums(wait_send, k)

        @when(k < HYBRID)
        def _():
            for n in range(CHUNK):
                wait_send_if(has_target[n], lambda: side_copy(k, n))
                wait_send_if(has_origin[n], lambda: back_copy(k, n))

    def step(k, _):
        ahead = k + AHEAD

        @pl.when((ahead >= max(AHEAD, HYBRID)) & (ahead < EARLY))
        def _():
            start(traces_low, traces_high, ahead, across)

        @pl.when(k < chunks - EARLY)
        def _():
            start(traces_low, traces_high, k + EARLY, along)

        @pl.when(k < HYBRID)
        def _():
            hybrid_gather(k)

        @pl.when((k >= HYBRID) & (k < EARLY))
        def _():
            gather(k, False)

        @pl.when((ahead >= EARLY) & (ahead < last))
        def _():
            gather(ahead, True)

        @pl.when(ahead == last)
        def _():
            gather_last()

        @pl.when((k >= LAG) & (k < last + LAG))
        def _():
            correlate(k - LAG)

        @pl.when(k >= SETTLE)
        def _():
            finish(k - SETTLE)

        return 0

    lax.fori_loop(0, last + LAG, step, 0)
    for k in range(last + LAG - SETTLE, chunks):
        finish(k)
    correlate_last()
    flush(channels // 8 - 1)
    for n in range(CHUNK):
        wait_send_if(has_left, lambda: tail_low(n))
        wait_send_if(has_right, lambda: tail_high(n))


def by_heading(pairs):
    return pairs.transpose(0, 2, 1, 3)[0]


def local(forward, inverse, traces, pair_first, pair_second, pair_valid):
    _, _, events, channels, samples = traces.shape
    chunks = channels // CHUNK
    part = pltpu.VMEM((channels, events, samples), F32)
    code = pltpu.VMEM((chunks, CHUNK * events * samples // 128 + 16, 128), jnp.int16)
    back = pltpu.VMEM((HYBRID, CHUNK * (events * LAGS // 128 + 16), 128), jnp.int16)
    tail = pltpu.VMEM((2, CHUNK, events * samples // 128 + 16, 128), jnp.int16)
    in_hbm = pl.BlockSpec(memory_space=pltpu.HBM)
    in_vmem = pl.BlockSpec(memory_space=pltpu.VMEM)
    dma = pltpu.SemaphoreType.DMA
    out = pl.pallas_call(
        kernel,
        out_shape=jax.ShapeDtypeStruct((events, channels, LAGS), F32),
        in_specs=[in_hbm, in_vmem, in_vmem, in_vmem, in_hbm, in_hbm],
        out_specs=in_vmem,
        scratch_shapes=[
            pltpu.VMEM((events, channels, samples), BF16),
            pltpu.VMEM((channels // 8, samples // 128, events * 8, 128), F32),
            pltpu.VMEM((channels, 3 * events, samples), BF16),
            part, code, code, code, code,
            pltpu.VMEM((HYBRID, CHUNK * events, samples), BF16),
            back, back, tail, tail,
            pltpu.VMEM((CHUNK * events, LAGS), F32),
            pltpu.VMEM((2, 3 * events, 3 * events), BF16),
            pltpu.VMEM((5, 16, 128), jnp.int32),
            pltpu.VMEM(forward.shape, BF16),
            pltpu.VMEM(inverse.shape, BF16),
            pltpu.VMEM((LAGS // 128, events * 8, 128), F32),
            dma, dma((2,)), dma((4,)), dma((4,)),
        ] + [dma((chunks,))] * 8 + [dma((HYBRID, CHUNK))] * 4 + [dma((2, CHUNK))] * 2,
        compiler_params=pltpu.CompilerParams(
            collective_id=0, has_side_effects=True, vmem_limit_bytes=40 * 1024 * 1024
        ),
        cost_estimate=pl.CostEstimate(
            flops=8 * 10**9, bytes_accessed=6 * 10**6, transcendentals=0
        ),
        name="event_correlation",
    )(*[pltpu.with_memory_space_constraint(v, pltpu.HBM) for v in (traces[0, 0], by_heading(pair_first), by_heading(pair_second), by_heading(pair_valid), forward, inverse)])
    return out[None, None]


def solution(mesh):
    forward, inverse = make_tables(512)
    spec4 = P("wide", "narrow", None, None)
    spec5 = P("wide", "narrow", None, None, None)

    def run(traces, pair_first, pair_second, pair_valid):
        return local(
            jnp.asarray(forward), jnp.asarray(inverse), traces, pair_first, pair_second, pair_valid
        )

    return jax.shard_map(
        run, mesh=mesh, in_specs=(spec5, spec4, spec4, spec4), out_specs=spec5, check_vma=False
    )
```

```python
import functools
import math

import jax
import jax.numpy as jnp
import ml_dtypes
import numpy as np
from jax import lax
from jax.experimental import pallas as pl
from jax.experimental.pallas import tpu as pltpu
from jax.sharding import PartitionSpec as P

LAGS = 256
BLOCK = 128
SHIFTS = (-1, 0, 1)
CHUNK = 2
LAG = 5
SETTLE = 8
FORWARD = 1
HYBRID = 5
EARLY = 8
AHEAD = 4
CODE_MAX = 32767.0
MESH = pl.DeviceIdType.MESH
F32 = jnp.float32
BF16 = jnp.bfloat16


def split_np(table):
    high = table.astype(ml_dtypes.bfloat16)
    low = (table - high.astype(np.float64)).astype(ml_dtypes.bfloat16)
    return np.stack([high, low])


def make_tables(samples):
    freq = np.arange(BLOCK, dtype=np.float64) + 0.5
    step = 2.0 * math.pi / (2 * BLOCK)
    phase = np.arange(BLOCK, dtype=np.float64)[:, None] * freq[None, :] * step
    forward = split_np(np.concatenate([np.cos(phase), -np.sin(phase)], axis=1))
    lag = np.arange(LAGS, dtype=np.float64) - LAGS // 2
    scale = 1.0 / (BLOCK * math.sqrt(samples))
    parts = []
    for d in SHIFTS:
        offset = lag - BLOCK * d
        phase = freq[:, None] * offset[None, :] * step
        inside = (np.abs(offset) < BLOCK)[None, :] * scale
        parts += [np.cos(phase) * inside, -np.sin(phase) * inside]
    return np.concatenate(list(forward), axis=0), split_np(np.concatenate(parts, axis=0))


def split(v):
    high = v.astype(BF16)
    return high, (v - high.astype(F32)).astype(BF16)


def dot(a, b):
    return jnp.dot(a, b, preferred_element_type=F32)


def when(condition):
    if isinstance(condition, bool):
        return (lambda body: body()) if condition else (lambda body: None)
    return pl.when(condition)


def kernel(
    traces, first, second, valid, fwd_hbm, inv_hbm, out,
    raw, wide32, cells, part_own, sent_low, sent_high, got_low, got_high,
    side, back_out, back_in, tail_out, tail_in, acc,
    weights, codes, fwd, inv, held,
    load_sem, table_sem, code_send, code_recv,
    x_send_low, x_send_high, x_from_low, x_from_high,
    y_send_low, y_send_high, y_from_low, y_from_high,
    side_send, side_recv, back_send, back_recv, tail_send, tail_recv,
):
    events, channels, samples = traces.shape
    lanes = samples // 128
    chunks = channels // CHUNK
    last = chunks - 1
    rows, cols = lax.axis_size("wide"), lax.axis_size("narrow")
    row, col = lax.axis_index("wide"), lax.axis_index("narrow")
    left = {"narrow": lax.rem(col + cols - 1, cols)}
    right = {"narrow": lax.rem(col + 1, cols)}
    up = {"wide": lax.rem(row + rows - 1, rows)}
    down = {"wide": lax.rem(row + 1, rows)}
    has_left, has_right = col > 0, col < cols - 1
    has_up, has_down = row > 0, row < rows - 1
    sides = ((has_left, left), (has_right, right), (has_up, up), (has_down, down))

    load = pltpu.make_async_copy(traces, raw, load_sem)
    load.start()
    barrier = pltpu.get_barrier_semaphore()
    for has, peer in sides:
        @pl.when(has)
        def _():
            pl.semaphore_signal(barrier, inc=1, device_id=peer, device_id_type=MESH)

    slots = first.shape[2]
    codes[0, 0:9, 0:slots] = jnp.where(
        valid[:, 0, :] == 1, first[:, 0, :] * events + second[:, 0, :], -1
    )

    def spread(group):
        for i in range(lanes):
            part = raw[:, group * 8 : (group + 1) * 8, i * 128 : (i + 1) * 128].astype(F32)
            wide32[group, i] = part.reshape(events * 8, 128)

    def turn(k):
        if k * CHUNK % 8 == 0:
            spread(k * CHUNK // 8)
        for c in range(k * CHUNK, (k + 1) * CHUNK):
            for i in range(lanes):
                lane_block = wide32[c // 8, i, pl.ds(c % 8, events, stride=8), :]
                cells[c, events : 2 * events, i * 128 : (i + 1) * 128] = lane_block.astype(BF16)

    back_rows = events * LAGS // 128

    def remote(src, dst, send, recv, peer):
        return pltpu.make_async_remote_copy(
            src_ref=src, dst_ref=dst, send_sem=send, recv_sem=recv,
            device_id=peer, device_id_type=MESH,
        )

    code_copies = [
        remote(codes.at[0], codes.at[slot], code_send.at[slot - 1], code_recv.at[slot - 1], peer)
        for slot, peer in ((2, left), (1, right), (4, up), (3, down))
    ]
    has_from = {1: has_left, 2: has_right, 3: has_up, 4: has_down}

    def traces_low(k, peer):
        block = pl.ds(k * CHUNK, CHUNK)
        return remote(
            cells.at[block, events : 2 * events, :], cells.at[block, 2 * events : 3 * events, :],
            x_send_low.at[k], x_from_high.at[k], peer,
        )

    def traces_high(k, peer):
        block = pl.ds(k * CHUNK, CHUNK)
        return remote(
            cells.at[block, events : 2 * events, :], cells.at[block, 0:events, :],
            x_send_high.at[k], x_from_low.at[k], peer,
        )

    def sums_low(k, peer):
        return remote(sent_low.at[k], got_high.at[k], y_send_low.at[k], y_from_high.at[k], peer)

    def sums_high(k, peer):
        return remote(sent_high.at[k], got_low.at[k], y_send_high.at[k], y_from_low.at[k], peer)

    across = ((has_left, left), (has_right, right))
    along = ((has_up, up), (has_down, down))

    def start(make_low, make_high, k, peers):
        (has_low, low), (has_high, high) = peers
        start_if(has_low, lambda: make_low(k, low))
        start_if(has_high, lambda: make_high(k, high))

    def wait_recv(make_low, make_high, k, peers):
        (has_low, low), (has_high, high) = peers
        wait_recv_if(has_low, lambda: make_high(k, high))
        wait_recv_if(has_high, lambda: make_low(k, low))

    def wait_send(make_low, make_high, k, peers):
        (has_low, low), (has_high, high) = peers
        wait_send_if(has_low, lambda: make_low(k, low))
        wait_send_if(has_high, lambda: make_high(k, high))

    def by_axis(act, make_low, make_high, k, is_across):
        @when(is_across)
        def _():
            act(make_low, make_high, k, across)

        @when(not is_across if isinstance(is_across, bool) else jnp.logical_not(is_across))
        def _():
            act(make_low, make_high, k, along)

    def on_traces(act, k):
        by_axis(act, traces_low, traces_high, k, (k >= HYBRID) & (k < EARLY))

    def on_sums(act, k):
        by_axis(act, sums_low, sums_high, k, k >= EARLY)

    def side_copy(k, n):
        return remote(
            cells.at[k * CHUNK + n, events : 2 * events, :],
            side.at[k, n * events : (n + 1) * events, :],
            side_send.at[k, n], side_recv.at[k, n], (right, left)[n],
        )

    def back_copy(pair, n, rows):
        return remote(
            back_out.at[pair, n, 0:rows, :], back_in.at[pair, n, 0:rows, :],
            back_send.at[pair, n], back_recv.at[pair, n], (left, right)[n],
        )

    def on_back(act, has, k, place):
        @when((k % 2 == place) & (k < HYBRID // 2 * 2))
        def _():
            for n in range(CHUNK):
                act(has[n], lambda: back_copy(k // 2, n, 2 * back_rows + 16))

        if HYBRID % 2:
            @when(k == HYBRID - 1)
            def _():
                for n in range(CHUNK):
                    act(has[n], lambda: back_copy(k // 2, n, back_rows + 16))

    has_target, has_origin = (has_right, has_left), (has_left, has_right)

    def start_if(has, make):
        @pl.when(has)
        def _():
            make().start()

    def wait_send_if(has, make):
        @pl.when(has)
        def _():
            make().wait_send()

    def wait_recv_if(has, make):
        @pl.when(has)
        def _():
            make().wait_recv()

    load.wait()
    load_fwd = pltpu.make_async_copy(fwd_hbm, fwd, table_sem.at[0])
    load_inv = pltpu.make_async_copy(inv_hbm, inv, table_sem.at[1])
    load_fwd.start()
    load_inv.start()

    turn(0)
    peers = sum(has.astype(jnp.int32) for has, _ in sides)
    pl.semaphore_wait(barrier, peers)
    for k in range(HYBRID):
        if k > 0:
            turn(k)
        for n in range(CHUNK):
            start_if(has_target[n], lambda: side_copy(k, n))
        if k == 0:
            for copy, (has, _) in zip(code_copies, sides):
                start_if(has, lambda: copy)
        on_traces(start, k)
    for k in range(HYBRID, chunks):
        turn(k)
    for k in range(EARLY, chunks):
        start(traces_low, traces_high, k, along)

    def blank(has, slot, block, span, first_row, row_count):
        @pl.when(jnp.logical_not(has))
        def _():
            codes[slot] = jnp.full(codes.shape[1:], -1, jnp.int32)

            def clear(n, _):
                block[n, first_row : first_row + row_count, :] = jnp.zeros(
                    (row_count, block.shape[2]), block.dtype
                )
                return 0

            lax.fori_loop(*span, clear, 0)

    hybrid_to, early_to = HYBRID * CHUNK, EARLY * CHUNK
    for span in ((0, hybrid_to), (early_to, channels)):
        blank(has_up, 3, cells, span, 0, events)
        blank(has_down, 4, cells, span, 2 * events, events)
    blank(has_left, 1, cells, (hybrid_to, early_to), 0, events)
    blank(has_right, 2, cells, (hybrid_to, early_to), 2 * events, events)
    blank(has_up, 3, got_low, (0, EARLY), 0, got_low.shape[1])
    blank(has_down, 4, got_high, (0, EARLY), 0, got_high.shape[1])
    blank(has_left, 1, got_low, (EARLY, last), 0, got_low.shape[1])
    blank(has_right, 2, got_high, (EARLY, last), 0, got_high.shape[1])
    blank(has_left, 1, tail_in.at[0], (0, CHUNK), 0, tail_in.shape[2])
    blank(has_right, 2, tail_in.at[1], (0, CHUNK), 0, tail_in.shape[2])
    blank(has_left, 1, side, (0, HYBRID), 0, events)
    blank(has_right, 2, side, (0, HYBRID), events, events)
    for pair in range(back_in.shape[0]):
        blank(has_right, 2, back_in.at[pair], (0, 1), 0, back_in.shape[2])
        blank(has_left, 1, back_in.at[pair], (1, 2), 0, back_in.shape[2])

    for copy, slot, (has, _) in zip(code_copies, (2, 1, 4, 3), sides):
        wait_send_if(has, lambda: copy)
        wait_recv_if(has_from[slot], lambda: copy)

    ids = lax.broadcasted_iota(jnp.int32, (events, slots), 0)

    def ends(slot, heading):
        code = codes[slot, heading : heading + 1, 0:slots]
        live = code >= 0
        head = jnp.where(live, code // events, -1)
        tail = jnp.where(live, code % events, -1)
        return (
            jnp.where(ids == head, 1.0, 0.0).astype(BF16),
            jnp.where(ids == tail, 1.0, 0.0).astype(BF16),
        )

    def outer(a, b):
        return lax.dot_general(
            a, b, (((1,), (1,)), ((), ())), preferred_element_type=F32
        )

    def count(target, target_heading, source, source_heading):
        head, tail = ends(target, target_heading)
        pairs = outer(head, tail)
        head, tail = ends(source, source_heading)
        return (pairs + outer(tail, head)).astype(BF16)

    by_row = {-1: 3, 0: 0, 1: 4}
    by_col = {-1: 1, 0: 0, 1: 2}
    for i in (-1, 0, 1):
        for j in (-1, 0, 1):
            rows_at = pl.ds((i + 1) * events, events)
            weights[0, rows_at, (j + 1) * events : (j + 2) * events] = count(
                by_row[i], (1 - i) * 3 + (j + 1), by_col[j], (i + 1) * 3 + (1 - j)
            )
            weights[1, rows_at, (j + 1) * events : (j + 2) * events] = count(
                by_col[i], (j + 1) * 3 + (1 - i), by_row[j], (1 - j) * 3 + (i + 1)
            )

    load_fwd.wait()
    load_inv.wait()

    size = CHUNK * events

    def diagonal(n):
        at = [lax.broadcasted_iota(jnp.int32, (n, n), dim) for dim in (0, 1)]
        return at[0] == at[1]

    def encoded(part):
        n = part.shape[0]
        peak = jnp.max(jnp.abs(part), axis=1, keepdims=True)
        power = jnp.ceil(jnp.log2(jnp.maximum(peak, 1e-30)) + 1e-4)
        code = jnp.round(part * (jnp.exp2(-power) * CODE_MAX))
        band = jnp.sum(jnp.where(diagonal(n), power, 0.0), axis=0, keepdims=True)
        band = jnp.broadcast_to(band, (16, n)).astype(jnp.int32).astype(jnp.int16)
        return code.astype(jnp.int32).astype(jnp.int16), band

    def encode(ref, at, part):
        n = part.shape[0]
        code, band = encoded(part)
        for i in range(lanes):
            ref[*at, i * n : (i + 1) * n, :] = code[:, i * 128 : (i + 1) * 128]
        ref[*at, lanes * n : lanes * n + 16, 0:n] = band

    def decode(ref, at, n):
        band = ref[*at, lanes * n : lanes * n + 16, 0:n].astype(jnp.int32).astype(F32)[0:1]
        power = jnp.sum(jnp.where(diagonal(n), band, 0.0), axis=1, keepdims=True)
        code = jnp.concatenate(
            [ref[*at, i * n : (i + 1) * n, :] for i in range(lanes)], axis=1
        ).astype(jnp.int32).astype(F32)
        return code * (jnp.exp2(power) * (1.0 / CODE_MAX))

    def gather(k, late):
        wait_recv(traces_low, traces_high, k, along if late else across)
        parts = [dot(weights[int(late)], cells[k * CHUNK + n]) for n in range(CHUNK)]
        for n in range(CHUNK):
            part_own[k * CHUNK + n] = parts[n][events : 2 * events]
        encode(sent_low, (k,), jnp.concatenate([p[0:events] for p in parts], axis=0))
        encode(sent_high, (k,), jnp.concatenate([p[2 * events :] for p in parts], axis=0))
        start(sums_low, sums_high, k, across if late else along)

    def correlation(x, y):
        size = x.shape[0]
        y_high, y_low = split(y)
        stack = []
        for v in (x, y_high, y_low):
            for i in range(lanes):
                block = v[:, i * BLOCK : (i + 1) * BLOCK]
                stack.append(jnp.concatenate([block, block], axis=1))
        spectra = dot(jnp.concatenate(stack, axis=0), fwd[...])
        spectra = [spectra[n * size : (n + 1) * size] for n in range(3 * lanes)]
        xs = spectra[:lanes]
        ys = [spectra[lanes + i] + spectra[2 * lanes + i] for i in range(lanes)]
        total = jnp.zeros((size, LAGS), F32)
        for n, d in enumerate(SHIFTS):
            real, imag = 0.0, 0.0
            for i in range(max(0, -d), min(lanes, lanes - d)):
                xr, xi = xs[i][:, :BLOCK], xs[i][:, BLOCK:]
                yr, yi = ys[i + d][:, :BLOCK], ys[i + d][:, BLOCK:]
                real = real + (xr * yr + xi * yi)
                imag = imag + (xr * yi - xi * yr)
            s_high, s_low = split(jnp.concatenate([real, imag], axis=1))
            span = slice(n * 2 * BLOCK, (n + 1) * 2 * BLOCK)
            both = dot(jnp.concatenate([s_high, s_low], axis=0), inv[0, span, :])
            total = total + (both[:size] + both[size:] + dot(s_high, inv[1, span, :]))
        return total

    def hybrid_gather(k):
        on_traces(wait_recv, k)
        for n in range(CHUNK):
            wait_recv_if(has_origin[n], lambda: side_copy(k, n))
        c = k * CHUNK
        column_first = dot(weights[1, 0 : 2 * events, :], cells[c])
        column_second = dot(weights[1, events : 3 * events, :], cells[c + 1])
        side_first = dot(weights[0, :, 0:events], side[k, 0:events, :])
        side_second = dot(weights[0, :, 2 * events : 3 * events], side[k, events : 2 * events, :])
        part_own[c] = column_first[events:] + side_first[events : 2 * events]
        part_own[c + 1] = column_second[0:events] + side_second[events : 2 * events]
        encode(sent_low, (k,), jnp.concatenate([side_first[0:events], side_second[0:events]], axis=0))
        encode(
            sent_high, (k,),
            jnp.concatenate([side_first[2 * events :], side_second[2 * events :]], axis=0),
        )
        on_sums(start, k)
        returned = jnp.concatenate([column_first[0:events], column_second[events:]], axis=0)
        code, band = encoded(correlation(side[k], returned))
        pair, half = k // 2, k % 2
        sublane = lax.broadcasted_iota(jnp.int32, (16, size), 0)
        for n in range(CHUNK):
            for i in range(LAGS // 128):
                at = pl.multiple_of(16 + half * back_rows + i * events, 16)
                back_out[pair, n, pl.ds(at, events), :] = code[
                    n * events : (n + 1) * events, i * 128 : (i + 1) * 128
                ]
            before = back_out[pair, n, 0:16, :].astype(jnp.int32)
            back_out[pair, n, 0:16, :] = jnp.where(
                sublane >= 8 * half, band.astype(jnp.int32), before
            ).astype(jnp.int16)
        on_back(start_if, has_origin, k, 1)

    def add_back(k):
        on_back(wait_recv_if, has_target, k, 0)
        pair, half = k // 2, k % 2
        bands = [back_in[pair, n, 0:16, :].astype(jnp.int32).astype(F32) for n in range(CHUNK)]
        lane = lax.broadcasted_iota(jnp.int32, (16, size), 1)
        band = jnp.where(lane < events, bands[0], bands[1])
        band = jnp.where(half == 0, band[0:1], band[8:9])
        power = jnp.sum(jnp.where(diagonal(size), band, 0.0), axis=1, keepdims=True)
        code = jnp.concatenate(
            [
                jnp.concatenate(
                    [
                        back_in[
                            pair, n,
                            pl.ds(
                                pl.multiple_of(16 + half * back_rows + i * events, 16), events
                            ),
                            :,
                        ]
                        for i in range(LAGS // 128)
                    ],
                    axis=1,
                )
                for n in range(CHUNK)
            ],
            axis=0,
        )
        acc[...] += code.astype(jnp.int32).astype(F32) * (jnp.exp2(power) * (1.0 / CODE_MAX))

    def tail_rows(n):
        return pl.ds(0, lanes * events + (16 if n == 0 else 0))

    def tail_low(n):
        return remote(
            tail_out.at[0, n, tail_rows(n)], tail_in.at[1, n, tail_rows(n)],
            tail_send.at[0, n], tail_recv.at[1, n], left,
        )

    def tail_high(n):
        return remote(
            tail_out.at[1, n, tail_rows(n)], tail_in.at[0, n, tail_rows(n)],
            tail_send.at[1, n], tail_recv.at[0, n], right,
        )

    def gather_last():
        wait_recv(traces_low, traces_high, last, along)
        parts = [dot(weights[1], cells[last * CHUNK + n]) for n in range(CHUNK)]
        for n in range(CHUNK):
            part_own[last * CHUNK + n] = parts[n][events : 2 * events]
        for way, first_row in ((0, 0), (1, 2 * events)):
            code, band = encoded(
                jnp.concatenate([p[first_row : first_row + events] for p in parts], axis=0)
            )
            for n in range(CHUNK):
                for i in range(lanes):
                    tail_out[way, n, i * events : (i + 1) * events, :] = code[
                        n * events : (n + 1) * events, i * 128 : (i + 1) * 128
                    ]
            tail_out[way, 0, lanes * events : lanes * events + 16, :] = band
        for n in range(CHUNK):
            start_if(has_left, lambda: tail_low(n))
            start_if(has_right, lambda: tail_high(n))

    def tail_part(way, n):
        band = tail_in[way, 0, lanes * events : lanes * events + 16, :]
        band = band.astype(jnp.int32).astype(F32)[0:1]
        power = jnp.sum(jnp.where(diagonal(size), band, 0.0), axis=1, keepdims=True)
        code = jnp.concatenate(
            [tail_in[way, n, i * events : (i + 1) * events, :] for i in range(lanes)], axis=1
        ).astype(jnp.int32).astype(F32)
        return code * (jnp.exp2(power[n * events : (n + 1) * events]) * (1.0 / CODE_MAX))

    def correlate_last():
        for n in range(CHUNK):
            c = last * CHUNK + n
            wait_recv_if(has_left, lambda: tail_high(n))
            wait_recv_if(has_right, lambda: tail_low(n))
            y = part_own[c] + tail_part(0, n) + tail_part(1, n)
            keep(c, correlation(cells[c, events : 2 * events, :], y))

    def keep(c, rows):
        for i in range(LAGS // 128):
            held[c // 8, i, pl.ds(c % 8, events, stride=8), :] = rows[:, i * 128 : (i + 1) * 128]

    def flush(group):
        place = pl.ds(group * 8, 8)
        for i in range(LAGS // 128):
            out[:, place, i * 128 : (i + 1) * 128] = held[group, i].reshape(events, 8, 128)

    def correlate(k):
        on_sums(wait_recv, k)
        block = pl.ds(k * CHUNK, CHUNK)
        x = cells[block, events : 2 * events, :].reshape(size, samples)
        y = part_own[block].reshape(size, samples) + decode(got_low, (k,), size) + decode(got_high, (k,), size)
        acc[...] = correlation(x, y)

        @pl.when(k < HYBRID)
        def _():
            add_back(k)

        total = acc[...]
        for n in range(CHUNK):
            keep(k * CHUNK + n, total[n * events : (n + 1) * events])

    def finish(k):
        on_traces(wait_send, k)

        @when(k < last)
        def _():
            on_sums(wait_send, k)

        @when(k < HYBRID)
        def _():
            for n in range(CHUNK):
                wait_send_if(has_target[n], lambda: side_copy(k, n))
            on_back(wait_send_if, has_origin, k, 1)

    def step(k, _):
        ahead = k + AHEAD

        @pl.when((ahead >= max(AHEAD, HYBRID)) & (ahead < EARLY))
        def _():
            start(traces_low, traces_high, ahead, across)

        @pl.when(k < HYBRID)
        def _():
            hybrid_gather(k)

        @pl.when((k >= HYBRID) & (k < EARLY))
        def _():
            gather(k, False)

        @pl.when((ahead >= EARLY) & (ahead < last))
        def _():
            gather(ahead, True)

        @pl.when(ahead == last)
        def _():
            gather_last()

        place = k - LAG
        moved = (place >= HYBRID) & (place < HYBRID + FORWARD)
        held_back = (place >= HYBRID + FORWARD) & (place < EARLY + FORWARD)

        @pl.when((place >= 0) & (place < last))
        def _():
            correlate(
                place
                + (EARLY - HYBRID) * moved.astype(jnp.int32)
                - FORWARD * held_back.astype(jnp.int32)
            )

        @pl.when(place == last - 1)
        def _():
            for group in range(channels // 8 - 1):
                flush(group)

        @pl.when(k >= SETTLE)
        def _():
            finish(k - SETTLE)

        return 0

    lax.fori_loop(0, last + LAG, step, 0)
    for k in range(last + LAG - SETTLE, chunks):
        finish(k)
    correlate_last()
    flush(channels // 8 - 1)
    for n in range(CHUNK):
        wait_send_if(has_left, lambda: tail_low(n))
        wait_send_if(has_right, lambda: tail_high(n))


def by_heading(pairs):
    return pairs.transpose(0, 2, 1, 3)[0]


def local(forward, inverse, traces, pair_first, pair_second, pair_valid):
    _, _, events, channels, samples = traces.shape
    chunks = channels // CHUNK
    part = pltpu.VMEM((channels, events, samples), F32)
    code = pltpu.VMEM((chunks, CHUNK * events * samples // 128 + 16, 128), jnp.int16)
    pairs = -(-HYBRID // 2)
    back = pltpu.VMEM((pairs, CHUNK, 2 * events * LAGS // 128 + 16, 128), jnp.int16)
    tail = pltpu.VMEM((2, CHUNK, events * samples // 128 + 16, 128), jnp.int16)
    in_hbm = pl.BlockSpec(memory_space=pltpu.HBM)
    in_vmem = pl.BlockSpec(memory_space=pltpu.VMEM)
    dma = pltpu.SemaphoreType.DMA
    out = pl.pallas_call(
        kernel,
        out_shape=jax.ShapeDtypeStruct((events, channels, LAGS), F32),
        in_specs=[in_hbm, in_vmem, in_vmem, in_vmem, in_hbm, in_hbm],
        out_specs=in_vmem,
        scratch_shapes=[
            pltpu.VMEM((events, channels, samples), BF16),
            pltpu.VMEM((channels // 8, samples // 128, events * 8, 128), F32),
            pltpu.VMEM((channels, 3 * events, samples), BF16),
            part, code, code, code, code,
            pltpu.VMEM((HYBRID, CHUNK * events, samples), BF16),
            back, back, tail, tail,
            pltpu.VMEM((CHUNK * events, LAGS), F32),
            pltpu.VMEM((2, 3 * events, 3 * events), BF16),
            pltpu.VMEM((5, 16, 128), jnp.int32),
            pltpu.VMEM(forward.shape, BF16),
            pltpu.VMEM(inverse.shape, BF16),
            pltpu.VMEM((channels // 8, LAGS // 128, events * 8, 128), F32),
            dma, dma((2,)), dma((4,)), dma((4,)),
        ] + [dma((chunks,))] * 8 + [dma((HYBRID, CHUNK))] * 2 + [dma((pairs, CHUNK))] * 2 + [dma((2, CHUNK))] * 2,
        compiler_params=pltpu.CompilerParams(
            collective_id=0, has_side_effects=True, vmem_limit_bytes=40 * 1024 * 1024
        ),
        cost_estimate=pl.CostEstimate(
            flops=8 * 10**9, bytes_accessed=6 * 10**6, transcendentals=0
        ),
        name="event_correlation",
    )(*[pltpu.with_memory_space_constraint(v, pltpu.HBM) for v in (traces[0, 0], by_heading(pair_first), by_heading(pair_second), by_heading(pair_valid), forward, inverse)])
    return out[None, None]


def solution(mesh):
    forward, inverse = make_tables(512)
    spec4 = P("wide", "narrow", None, None)
    spec5 = P("wide", "narrow", None, None, None)

    def run(traces, pair_first, pair_second, pair_valid):
        return local(
            jnp.asarray(forward), jnp.asarray(inverse), traces, pair_first, pair_second, pair_valid
        )

    return jax.shard_map(
        run, mesh=mesh, in_specs=(spec5, spec4, spec4, spec4), out_specs=spec5, check_vma=False
    )
```

```python
import functools
import math

import jax
import jax.numpy as jnp
import ml_dtypes
import numpy as np
from jax import lax
from jax.experimental import pallas as pl
from jax.experimental.pallas import tpu as pltpu
from jax.sharding import PartitionSpec as P

LAGS = 256
BLOCK = 128
SHIFTS = (-1, 0, 1)
CHUNK = 2
LAG = 5
SETTLE = 8
FORWARD = 1
LOADS = 4
HYBRID = 5
EARLY = 8
AHEAD = 4
CODE_MAX = 32767.0
MESH = pl.DeviceIdType.MESH
F32 = jnp.float32
BF16 = jnp.bfloat16


def split_np(table):
    high = table.astype(ml_dtypes.bfloat16)
    low = (table - high.astype(np.float64)).astype(ml_dtypes.bfloat16)
    return np.stack([high, low])


def make_tables(samples):
    freq = np.arange(BLOCK, dtype=np.float64) + 0.5
    step = 2.0 * math.pi / (2 * BLOCK)
    phase = np.arange(BLOCK, dtype=np.float64)[:, None] * freq[None, :] * step
    forward = split_np(np.concatenate([np.cos(phase), -np.sin(phase)], axis=1))
    lag = np.arange(LAGS, dtype=np.float64) - LAGS // 2
    scale = 1.0 / (BLOCK * math.sqrt(samples))
    parts = []
    for d in SHIFTS:
        offset = lag - BLOCK * d
        phase = freq[:, None] * offset[None, :] * step
        inside = (np.abs(offset) < BLOCK)[None, :] * scale
        parts += [np.cos(phase) * inside, -np.sin(phase) * inside]
    return np.concatenate(list(forward), axis=0), split_np(np.concatenate(parts, axis=0))


def split(v):
    high = v.astype(BF16)
    return high, (v - high.astype(F32)).astype(BF16)


def dot(a, b):
    return jnp.dot(a, b, preferred_element_type=F32)


def when(condition):
    if isinstance(condition, bool):
        return (lambda body: body()) if condition else (lambda body: None)
    return pl.when(condition)


def kernel(
    traces, first, second, valid, fwd_hbm, inv_hbm, out,
    raw, wide32, cells, part_own, sent_low, sent_high, got_low, got_high,
    side, back_out, back_in, tail_out, tail_in, acc,
    weights, codes, fwd, inv, held,
    load_sem, table_sem, code_send, code_recv,
    x_send_low, x_send_high, x_from_low, x_from_high,
    y_send_low, y_send_high, y_from_low, y_from_high,
    side_send, side_recv, back_send, back_recv, tail_send, tail_recv,
):
    events, channels, samples = traces.shape
    lanes = samples // 128
    chunks = channels // CHUNK
    last = chunks - 1
    rows, cols = lax.axis_size("wide"), lax.axis_size("narrow")
    row, col = lax.axis_index("wide"), lax.axis_index("narrow")
    left = {"narrow": lax.rem(col + cols - 1, cols)}
    right = {"narrow": lax.rem(col + 1, cols)}
    up = {"wide": lax.rem(row + rows - 1, rows)}
    down = {"wide": lax.rem(row + 1, rows)}
    has_left, has_right = col > 0, col < cols - 1
    has_up, has_down = row > 0, row < rows - 1
    sides = ((has_left, left), (has_right, right), (has_up, up), (has_down, down))

    share = events // LOADS
    loads = [
        pltpu.make_async_copy(
            traces.at[i * share : (i + 1) * share], raw.at[i * share : (i + 1) * share],
            load_sem.at[i],
        )
        for i in range(LOADS)
    ]
    for load in loads:
        load.start()
    barrier = pltpu.get_barrier_semaphore()
    for has, peer in sides:
        @pl.when(has)
        def _():
            pl.semaphore_signal(barrier, inc=1, device_id=peer, device_id_type=MESH)

    slots = first.shape[2]
    codes[0, 0:9, 0:slots] = jnp.where(
        valid[:, 0, :] == 1, first[:, 0, :] * events + second[:, 0, :], -1
    )

    def spread(group):
        for i in range(lanes):
            part = raw[:, group * 8 : (group + 1) * 8, i * 128 : (i + 1) * 128].astype(F32)
            wide32[group, i] = part.reshape(events * 8, 128)

    def turn(k):
        if k * CHUNK % 8 == 0:
            spread(k * CHUNK // 8)
        for c in range(k * CHUNK, (k + 1) * CHUNK):
            for i in range(lanes):
                lane_block = wide32[c // 8, i, pl.ds(c % 8, events, stride=8), :]
                cells[c, events : 2 * events, i * 128 : (i + 1) * 128] = lane_block.astype(BF16)

    back_rows = events * LAGS // 128

    def remote(src, dst, send, recv, peer):
        return pltpu.make_async_remote_copy(
            src_ref=src, dst_ref=dst, send_sem=send, recv_sem=recv,
            device_id=peer, device_id_type=MESH,
        )

    code_copies = [
        remote(codes.at[0], codes.at[slot], code_send.at[slot - 1], code_recv.at[slot - 1], peer)
        for slot, peer in ((2, left), (1, right), (4, up), (3, down))
    ]
    has_from = {1: has_left, 2: has_right, 3: has_up, 4: has_down}

    def traces_low(k, peer):
        block = pl.ds(k * CHUNK, CHUNK)
        return remote(
            cells.at[block, events : 2 * events, :], cells.at[block, 2 * events : 3 * events, :],
            x_send_low.at[k], x_from_high.at[k], peer,
        )

    def traces_high(k, peer):
        block = pl.ds(k * CHUNK, CHUNK)
        return remote(
            cells.at[block, events : 2 * events, :], cells.at[block, 0:events, :],
            x_send_high.at[k], x_from_low.at[k], peer,
        )

    def sums_low(k, peer):
        return remote(sent_low.at[k], got_high.at[k], y_send_low.at[k], y_from_high.at[k], peer)

    def sums_high(k, peer):
        return remote(sent_high.at[k], got_low.at[k], y_send_high.at[k], y_from_low.at[k], peer)

    across = ((has_left, left), (has_right, right))
    along = ((has_up, up), (has_down, down))

    def start(make_low, make_high, k, peers):
        (has_low, low), (has_high, high) = peers
        start_if(has_low, lambda: make_low(k, low))
        start_if(has_high, lambda: make_high(k, high))

    def wait_recv(make_low, make_high, k, peers):
        (has_low, low), (has_high, high) = peers
        wait_recv_if(has_low, lambda: make_high(k, high))
        wait_recv_if(has_high, lambda: make_low(k, low))

    def wait_send(make_low, make_high, k, peers):
        (has_low, low), (has_high, high) = peers
        wait_send_if(has_low, lambda: make_low(k, low))
        wait_send_if(has_high, lambda: make_high(k, high))

    def by_axis(act, make_low, make_high, k, is_across):
        @when(is_across)
        def _():
            act(make_low, make_high, k, across)

        @when(not is_across if isinstance(is_across, bool) else jnp.logical_not(is_across))
        def _():
            act(make_low, make_high, k, along)

    def on_traces(act, k):
        by_axis(act, traces_low, traces_high, k, (k >= HYBRID) & (k < EARLY))

    def on_sums(act, k):
        by_axis(act, sums_low, sums_high, k, k >= EARLY)

    def side_copy(k, n):
        return remote(
            cells.at[k * CHUNK + n, events : 2 * events, :],
            side.at[k, n * events : (n + 1) * events, :],
            side_send.at[k, n], side_recv.at[k, n], (right, left)[n],
        )

    def back_copy(pair, n, rows):
        return remote(
            back_out.at[pair, n, 0:rows, :], back_in.at[pair, n, 0:rows, :],
            back_send.at[pair, n], back_recv.at[pair, n], (left, right)[n],
        )

    def on_back(act, has, k, place):
        @when((k % 2 == place) & (k < HYBRID // 2 * 2))
        def _():
            for n in range(CHUNK):
                act(has[n], lambda: back_copy(k // 2, n, 2 * back_rows + 16))

        if HYBRID % 2:
            @when(k == HYBRID - 1)
            def _():
                for n in range(CHUNK):
                    act(has[n], lambda: back_copy(k // 2, n, back_rows + 16))

    has_target, has_origin = (has_right, has_left), (has_left, has_right)

    def start_if(has, make):
        @pl.when(has)
        def _():
            make().start()

    def wait_send_if(has, make):
        @pl.when(has)
        def _():
            make().wait_send()

    def wait_recv_if(has, make):
        @pl.when(has)
        def _():
            make().wait_recv()

    for load in loads:
        load.wait()
    load_fwd = pltpu.make_async_copy(fwd_hbm, fwd, table_sem.at[0])
    load_inv = pltpu.make_async_copy(inv_hbm, inv, table_sem.at[1])
    load_fwd.start()
    load_inv.start()

    turn(0)
    peers = sum(has.astype(jnp.int32) for has, _ in sides)
    pl.semaphore_wait(barrier, peers)
    for k in range(HYBRID):
        if k > 0:
            turn(k)
        for n in range(CHUNK):
            start_if(has_target[n], lambda: side_copy(k, n))
        if k == 0:
            for copy, (has, _) in zip(code_copies, sides):
                start_if(has, lambda: copy)
        on_traces(start, k)
    for k in range(HYBRID, chunks):
        turn(k)
    for k in range(EARLY, chunks):
        start(traces_low, traces_high, k, along)
    start(traces_low, traces_high, HYBRID, across)

    def blank(has, slot, block, span, first_row, row_count):
        @pl.when(jnp.logical_not(has))
        def _():
            codes[slot] = jnp.full(codes.shape[1:], -1, jnp.int32)

            def clear(n, _):
                block[n, first_row : first_row + row_count, :] = jnp.zeros(
                    (row_count, block.shape[2]), block.dtype
                )
                return 0

            lax.fori_loop(*span, clear, 0)

    hybrid_to, early_to = HYBRID * CHUNK, EARLY * CHUNK
    for span in ((0, hybrid_to), (early_to, channels)):
        blank(has_up, 3, cells, span, 0, events)
        blank(has_down, 4, cells, span, 2 * events, events)
    blank(has_left, 1, cells, (hybrid_to, early_to), 0, events)
    blank(has_right, 2, cells, (hybrid_to, early_to), 2 * events, events)
    blank(has_up, 3, got_low, (0, EARLY), 0, got_low.shape[1])
    blank(has_down, 4, got_high, (0, EARLY), 0, got_high.shape[1])
    blank(has_left, 1, got_low, (EARLY, last), 0, got_low.shape[1])
    blank(has_right, 2, got_high, (EARLY, last), 0, got_high.shape[1])
    blank(has_left, 1, tail_in.at[0], (0, CHUNK), 0, tail_in.shape[2])
    blank(has_right, 2, tail_in.at[1], (0, CHUNK), 0, tail_in.shape[2])
    blank(has_left, 1, side, (0, HYBRID), 0, events)
    blank(has_right, 2, side, (0, HYBRID), events, events)
    for pair in range(back_in.shape[0]):
        blank(has_right, 2, back_in.at[pair], (0, 1), 0, back_in.shape[2])
        blank(has_left, 1, back_in.at[pair], (1, 2), 0, back_in.shape[2])

    for copy, slot, (has, _) in zip(code_copies, (2, 1, 4, 3), sides):
        wait_send_if(has, lambda: copy)
        wait_recv_if(has_from[slot], lambda: copy)

    ids = lax.broadcasted_iota(jnp.int32, (events, slots), 0)

    def ends(slot, heading):
        code = codes[slot, heading : heading + 1, 0:slots]
        live = code >= 0
        head = jnp.where(live, code // events, -1)
        tail = jnp.where(live, code % events, -1)
        return (
            jnp.where(ids == head, 1.0, 0.0).astype(BF16),
            jnp.where(ids == tail, 1.0, 0.0).astype(BF16),
        )

    def outer(a, b):
        return lax.dot_general(
            a, b, (((1,), (1,)), ((), ())), preferred_element_type=F32
        )

    def count(target, target_heading, source, source_heading):
        head, tail = ends(target, target_heading)
        pairs = outer(head, tail)
        head, tail = ends(source, source_heading)
        return (pairs + outer(tail, head)).astype(BF16)

    by_row = {-1: 3, 0: 0, 1: 4}
    by_col = {-1: 1, 0: 0, 1: 2}
    for i in (-1, 0, 1):
        for j in (-1, 0, 1):
            rows_at = pl.ds((i + 1) * events, events)
            weights[0, rows_at, (j + 1) * events : (j + 2) * events] = count(
                by_row[i], (1 - i) * 3 + (j + 1), by_col[j], (i + 1) * 3 + (1 - j)
            )
            weights[1, rows_at, (j + 1) * events : (j + 2) * events] = count(
                by_col[i], (j + 1) * 3 + (1 - i), by_row[j], (1 - j) * 3 + (i + 1)
            )

    load_fwd.wait()
    load_inv.wait()

    size = CHUNK * events

    def diagonal(n):
        at = [lax.broadcasted_iota(jnp.int32, (n, n), dim) for dim in (0, 1)]
        return at[0] == at[1]

    def encoded(part):
        n = part.shape[0]
        peak = jnp.max(jnp.abs(part), axis=1, keepdims=True)
        power = jnp.ceil(jnp.log2(jnp.maximum(peak, 1e-30)) + 1e-4)
        code = jnp.round(part * (jnp.exp2(-power) * CODE_MAX))
        band = jnp.sum(jnp.where(diagonal(n), power, 0.0), axis=0, keepdims=True)
        band = jnp.broadcast_to(band, (16, n)).astype(jnp.int32).astype(jnp.int16)
        return code.astype(jnp.int32).astype(jnp.int16), band

    def encode(ref, at, part):
        n = part.shape[0]
        code, band = encoded(part)
        for i in range(lanes):
            ref[*at, i * n : (i + 1) * n, :] = code[:, i * 128 : (i + 1) * 128]
        ref[*at, lanes * n : lanes * n + 16, 0:n] = band

    def decode(ref, at, n):
        band = ref[*at, lanes * n : lanes * n + 16, 0:n].astype(jnp.int32).astype(F32)[0:1]
        power = jnp.sum(jnp.where(diagonal(n), band, 0.0), axis=1, keepdims=True)
        code = jnp.concatenate(
            [ref[*at, i * n : (i + 1) * n, :] for i in range(lanes)], axis=1
        ).astype(jnp.int32).astype(F32)
        return code * (jnp.exp2(power) * (1.0 / CODE_MAX))

    def gather(k, late):
        wait_recv(traces_low, traces_high, k, along if late else across)
        parts = [dot(weights[int(late)], cells[k * CHUNK + n]) for n in range(CHUNK)]
        for n in range(CHUNK):
            part_own[k * CHUNK + n] = parts[n][events : 2 * events]
        encode(sent_low, (k,), jnp.concatenate([p[0:events] for p in parts], axis=0))
        encode(sent_high, (k,), jnp.concatenate([p[2 * events :] for p in parts], axis=0))
        start(sums_low, sums_high, k, across if late else along)

    def correlation(x, y):
        size = x.shape[0]
        y_high, y_low = split(y)
        stack = []
        for v in (x, y_high, y_low):
            for i in range(lanes):
                block = v[:, i * BLOCK : (i + 1) * BLOCK]
                stack.append(jnp.concatenate([block, block], axis=1))
        spectra = dot(jnp.concatenate(stack, axis=0), fwd[...])
        spectra = [spectra[n * size : (n + 1) * size] for n in range(3 * lanes)]
        xs = spectra[:lanes]
        ys = [spectra[lanes + i] + spectra[2 * lanes + i] for i in range(lanes)]
        total = jnp.zeros((size, LAGS), F32)
        for n, d in enumerate(SHIFTS):
            real, imag = 0.0, 0.0
            for i in range(max(0, -d), min(lanes, lanes - d)):
                xr, xi = xs[i][:, :BLOCK], xs[i][:, BLOCK:]
                yr, yi = ys[i + d][:, :BLOCK], ys[i + d][:, BLOCK:]
                real = real + (xr * yr + xi * yi)
                imag = imag + (xr * yi - xi * yr)
            s_high, s_low = split(jnp.concatenate([real, imag], axis=1))
            span = slice(n * 2 * BLOCK, (n + 1) * 2 * BLOCK)
            both = dot(jnp.concatenate([s_high, s_low], axis=0), inv[0, span, :])
            total = total + (both[:size] + both[size:] + dot(s_high, inv[1, span, :]))
        return total

    def hybrid_gather(k):
        on_traces(wait_recv, k)
        for n in range(CHUNK):
            wait_recv_if(has_origin[n], lambda: side_copy(k, n))
        c = k * CHUNK
        column_first = dot(weights[1, 0 : 2 * events, :], cells[c])
        column_second = dot(weights[1, events : 3 * events, :], cells[c + 1])
        side_first = dot(weights[0, :, 0:events], side[k, 0:events, :])
        side_second = dot(weights[0, :, 2 * events : 3 * events], side[k, events : 2 * events, :])
        part_own[c] = column_first[events:] + side_first[events : 2 * events]
        part_own[c + 1] = column_second[0:events] + side_second[events : 2 * events]
        encode(sent_low, (k,), jnp.concatenate([side_first[0:events], side_second[0:events]], axis=0))
        encode(
            sent_high, (k,),
            jnp.concatenate([side_first[2 * events :], side_second[2 * events :]], axis=0),
        )
        on_sums(start, k)
        returned = jnp.concatenate([column_first[0:events], column_second[events:]], axis=0)
        code, band = encoded(correlation(side[k], returned))
        pair, half = k // 2, k % 2
        sublane = lax.broadcasted_iota(jnp.int32, (16, size), 0)
        for n in range(CHUNK):
            for i in range(LAGS // 128):
                at = pl.multiple_of(16 + half * back_rows + i * events, 16)
                back_out[pair, n, pl.ds(at, events), :] = code[
                    n * events : (n + 1) * events, i * 128 : (i + 1) * 128
                ]
            before = back_out[pair, n, 0:16, :].astype(jnp.int32)
            back_out[pair, n, 0:16, :] = jnp.where(
                sublane >= 8 * half, band.astype(jnp.int32), before
            ).astype(jnp.int16)
        on_back(start_if, has_origin, k, 1)

    def add_back(k):
        on_back(wait_recv_if, has_target, k, 0)
        pair, half = k // 2, k % 2
        bands = [back_in[pair, n, 0:16, :].astype(jnp.int32).astype(F32) for n in range(CHUNK)]
        lane = lax.broadcasted_iota(jnp.int32, (16, size), 1)
        band = jnp.where(lane < events, bands[0], bands[1])
        band = jnp.where(half == 0, band[0:1], band[8:9])
        power = jnp.sum(jnp.where(diagonal(size), band, 0.0), axis=1, keepdims=True)
        code = jnp.concatenate(
            [
                jnp.concatenate(
                    [
                        back_in[
                            pair, n,
                            pl.ds(
                                pl.multiple_of(16 + half * back_rows + i * events, 16), events
                            ),
                            :,
                        ]
                        for i in range(LAGS // 128)
                    ],
                    axis=1,
                )
                for n in range(CHUNK)
            ],
            axis=0,
        )
        acc[...] += code.astype(jnp.int32).astype(F32) * (jnp.exp2(power) * (1.0 / CODE_MAX))

    def tail_rows(n):
        return pl.ds(0, lanes * events + (16 if n == 0 else 0))

    def tail_low(n):
        return remote(
            tail_out.at[0, n, tail_rows(n)], tail_in.at[1, n, tail_rows(n)],
            tail_send.at[0, n], tail_recv.at[1, n], left,
        )

    def tail_high(n):
        return remote(
            tail_out.at[1, n, tail_rows(n)], tail_in.at[0, n, tail_rows(n)],
            tail_send.at[1, n], tail_recv.at[0, n], right,
        )

    def gather_last():
        wait_recv(traces_low, traces_high, last, along)
        parts = [dot(weights[1], cells[last * CHUNK + n]) for n in range(CHUNK)]
        for n in range(CHUNK):
            part_own[last * CHUNK + n] = parts[n][events : 2 * events]
        for way, first_row in ((0, 0), (1, 2 * events)):
            code, band = encoded(
                jnp.concatenate([p[first_row : first_row + events] for p in parts], axis=0)
            )
            for n in range(CHUNK):
                for i in range(lanes):
                    tail_out[way, n, i * events : (i + 1) * events, :] = code[
                        n * events : (n + 1) * events, i * 128 : (i + 1) * 128
                    ]
            tail_out[way, 0, lanes * events : lanes * events + 16, :] = band
        for n in range(CHUNK):
            start_if(has_left, lambda: tail_low(n))
            start_if(has_right, lambda: tail_high(n))

    def tail_part(way, n):
        band = tail_in[way, 0, lanes * events : lanes * events + 16, :]
        band = band.astype(jnp.int32).astype(F32)[0:1]
        power = jnp.sum(jnp.where(diagonal(size), band, 0.0), axis=1, keepdims=True)
        code = jnp.concatenate(
            [tail_in[way, n, i * events : (i + 1) * events, :] for i in range(lanes)], axis=1
        ).astype(jnp.int32).astype(F32)
        return code * (jnp.exp2(power[n * events : (n + 1) * events]) * (1.0 / CODE_MAX))

    def correlate_last():
        for n in range(CHUNK):
            c = last * CHUNK + n
            wait_recv_if(has_left, lambda: tail_high(n))
            wait_recv_if(has_right, lambda: tail_low(n))
            y = part_own[c] + tail_part(0, n) + tail_part(1, n)
            keep(c, correlation(cells[c, events : 2 * events, :], y))

    def keep(c, rows):
        for i in range(LAGS // 128):
            held[c // 8, i, pl.ds(c % 8, events, stride=8), :] = rows[:, i * 128 : (i + 1) * 128]

    def flush(group):
        place = pl.ds(group * 8, 8)
        for i in range(LAGS // 128):
            out[:, place, i * 128 : (i + 1) * 128] = held[group, i].reshape(events, 8, 128)

    def correlate(k):
        on_sums(wait_recv, k)
        block = pl.ds(k * CHUNK, CHUNK)
        x = cells[block, events : 2 * events, :].reshape(size, samples)
        y = part_own[block].reshape(size, samples) + decode(got_low, (k,), size) + decode(got_high, (k,), size)
        acc[...] = correlation(x, y)

        @pl.when(k < HYBRID)
        def _():
            add_back(k)

        total = acc[...]
        for n in range(CHUNK):
            keep(k * CHUNK + n, total[n * events : (n + 1) * events])

    def finish(k):
        on_traces(wait_send, k)

        @when(k < last)
        def _():
            on_sums(wait_send, k)

        @when(k < HYBRID)
        def _():
            for n in range(CHUNK):
                wait_send_if(has_target[n], lambda: side_copy(k, n))
            on_back(wait_send_if, has_origin, k, 1)

    def step(k, _):
        ahead = k + AHEAD

        @pl.when((k >= 2) & (k < EARLY - HYBRID - 1 + 2))
        def _():
            start(traces_low, traces_high, k + HYBRID + 1 - 2, across)

        @pl.when(k < HYBRID)
        def _():
            hybrid_gather(k)

        @pl.when((k >= HYBRID) & (k < EARLY))
        def _():
            gather(k, False)

        @pl.when((ahead >= EARLY) & (ahead < last))
        def _():
            gather(ahead, True)

        @pl.when(ahead == last)
        def _():
            gather_last()

        place = k - LAG
        moved = (place >= HYBRID) & (place < HYBRID + FORWARD)
        held_back = (place >= HYBRID + FORWARD) & (place < EARLY + FORWARD)

        @pl.when((place >= 0) & (place < last))
        def _():
            correlate(
                place
                + (EARLY - HYBRID) * moved.astype(jnp.int32)
                - FORWARD * held_back.astype(jnp.int32)
            )

        @pl.when(place == last - 1)
        def _():
            for group in range(channels // 8 - 1):
                flush(group)

        @pl.when(k >= SETTLE)
        def _():
            finish(k - SETTLE)

        return 0

    lax.fori_loop(0, last + LAG, step, 0)
    for k in range(last + LAG - SETTLE, chunks):
        finish(k)
    correlate_last()
    flush(channels // 8 - 1)
    for n in range(CHUNK):
        wait_send_if(has_left, lambda: tail_low(n))
        wait_send_if(has_right, lambda: tail_high(n))


def by_heading(pairs):
    return pairs.transpose(0, 2, 1, 3)[0]


def local(forward, inverse, traces, pair_first, pair_second, pair_valid):
    _, _, events, channels, samples = traces.shape
    chunks = channels // CHUNK
    part = pltpu.VMEM((channels, events, samples), F32)
    code = pltpu.VMEM((chunks, CHUNK * events * samples // 128 + 16, 128), jnp.int16)
    pairs = -(-HYBRID // 2)
    back = pltpu.VMEM((pairs, CHUNK, 2 * events * LAGS // 128 + 16, 128), jnp.int16)
    tail = pltpu.VMEM((2, CHUNK, events * samples // 128 + 16, 128), jnp.int16)
    in_hbm = pl.BlockSpec(memory_space=pltpu.HBM)
    in_vmem = pl.BlockSpec(memory_space=pltpu.VMEM)
    dma = pltpu.SemaphoreType.DMA
    out = pl.pallas_call(
        kernel,
        out_shape=jax.ShapeDtypeStruct((events, channels, LAGS), F32),
        in_specs=[in_hbm, in_vmem, in_vmem, in_vmem, in_hbm, in_hbm],
        out_specs=in_vmem,
        scratch_shapes=[
            pltpu.VMEM((events, channels, samples), BF16),
            pltpu.VMEM((channels // 8, samples // 128, events * 8, 128), F32),
            pltpu.VMEM((channels, 3 * events, samples), BF16),
            part, code, code, code, code,
            pltpu.VMEM((HYBRID, CHUNK * events, samples), BF16),
            back, back, tail, tail,
            pltpu.VMEM((CHUNK * events, LAGS), F32),
            pltpu.VMEM((2, 3 * events, 3 * events), BF16),
            pltpu.VMEM((5, 16, 128), jnp.int32),
            pltpu.VMEM(forward.shape, BF16),
            pltpu.VMEM(inverse.shape, BF16),
            pltpu.VMEM((channels // 8, LAGS // 128, events * 8, 128), F32),
            dma((LOADS,)), dma((2,)), dma((4,)), dma((4,)),
        ] + [dma((chunks,))] * 8 + [dma((HYBRID, CHUNK))] * 2 + [dma((pairs, CHUNK))] * 2 + [dma((2, CHUNK))] * 2,
        compiler_params=pltpu.CompilerParams(
            collective_id=0, has_side_effects=True, vmem_limit_bytes=40 * 1024 * 1024
        ),
        cost_estimate=pl.CostEstimate(
            flops=8 * 10**9, bytes_accessed=6 * 10**6, transcendentals=0
        ),
        name="event_correlation",
    )(*[pltpu.with_memory_space_constraint(v, pltpu.HBM) for v in (traces[0, 0], by_heading(pair_first), by_heading(pair_second), by_heading(pair_valid), forward, inverse)])
    return out[None, None]


def solution(mesh):
    forward, inverse = make_tables(512)
    spec4 = P("wide", "narrow", None, None)
    spec5 = P("wide", "narrow", None, None, None)

    def run(traces, pair_first, pair_second, pair_valid):
        return local(
            jnp.asarray(forward), jnp.asarray(inverse), traces, pair_first, pair_second, pair_valid
        )

    return jax.shard_map(
        run, mesh=mesh, in_specs=(spec5, spec4, spec4, spec4), out_specs=spec5, check_vma=False
    )
```

```python
import functools
import math

import jax
import jax.numpy as jnp
import ml_dtypes
import numpy as np
from jax import lax
from jax.experimental import pallas as pl
from jax.experimental.pallas import tpu as pltpu
from jax.sharding import PartitionSpec as P

LAGS = 256
BLOCK = 128
SHIFTS = (-1, 0, 1)
CHUNK = 2
LAG = 5
SETTLE = 8
FORWARD = 1
LOADS = 4
HYBRID = 5
EARLY = 8
AHEAD = 4
CODE_MAX = 32767.0
MESH = pl.DeviceIdType.MESH
F32 = jnp.float32
BF16 = jnp.bfloat16


def split_np(table):
    high = table.astype(ml_dtypes.bfloat16)
    low = (table - high.astype(np.float64)).astype(ml_dtypes.bfloat16)
    return np.stack([high, low])


def make_tables(samples):
    freq = np.arange(BLOCK, dtype=np.float64) + 0.5
    step = 2.0 * math.pi / (2 * BLOCK)
    phase = np.arange(BLOCK, dtype=np.float64)[:, None] * freq[None, :] * step
    forward = split_np(np.concatenate([np.cos(phase), -np.sin(phase)], axis=1))
    lag = np.arange(LAGS, dtype=np.float64) - LAGS // 2
    scale = 1.0 / (BLOCK * math.sqrt(samples))
    parts = []
    for d in SHIFTS:
        offset = lag - BLOCK * d
        phase = freq[:, None] * offset[None, :] * step
        inside = (np.abs(offset) < BLOCK)[None, :] * scale
        parts += [np.cos(phase) * inside, -np.sin(phase) * inside]
    return np.concatenate(list(forward), axis=0), split_np(np.concatenate(parts, axis=0))


def split(v):
    high = v.astype(BF16)
    return high, (v - high.astype(F32)).astype(BF16)


def dot(a, b):
    return jnp.dot(a, b, preferred_element_type=F32)


def when(condition):
    if isinstance(condition, bool):
        return (lambda body: body()) if condition else (lambda body: None)
    return pl.when(condition)


def kernel(
    traces, first, second, valid, fwd_hbm, inv_hbm, out,
    raw, wide32, cells, part_own, sent_low, sent_high, got_low, got_high,
    side, back_out, back_in, tail_out, tail_in, acc,
    weights, codes, fwd, inv, held,
    load_sem, table_sem, code_send, code_recv,
    x_send_low, x_send_high, x_from_low, x_from_high,
    y_send_low, y_send_high, y_from_low, y_from_high,
    side_send, side_recv, back_send, back_recv, tail_send, tail_recv,
):
    events, channels, samples = traces.shape
    lanes = samples // 128
    chunks = channels // CHUNK
    last = chunks - 1
    rows, cols = lax.axis_size("wide"), lax.axis_size("narrow")
    row, col = lax.axis_index("wide"), lax.axis_index("narrow")
    left = {"narrow": lax.rem(col + cols - 1, cols)}
    right = {"narrow": lax.rem(col + 1, cols)}
    up = {"wide": lax.rem(row + rows - 1, rows)}
    down = {"wide": lax.rem(row + 1, rows)}
    has_left, has_right = col > 0, col < cols - 1
    has_up, has_down = row > 0, row < rows - 1
    sides = ((has_left, left), (has_right, right), (has_up, up), (has_down, down))

    share = events // LOADS
    loads = [
        pltpu.make_async_copy(
            traces.at[i * share : (i + 1) * share], raw.at[i * share : (i + 1) * share],
            load_sem.at[i],
        )
        for i in range(LOADS)
    ]
    for load in loads:
        load.start()
    barrier = pltpu.get_barrier_semaphore()
    for has, peer in sides:
        @pl.when(has)
        def _():
            pl.semaphore_signal(barrier, inc=1, device_id=peer, device_id_type=MESH)

    slots = first.shape[2]
    codes[0, 0:9, 0:slots] = jnp.where(
        valid[:, 0, :] == 1, first[:, 0, :] * events + second[:, 0, :], -1
    )

    def spread(group):
        for i in range(lanes):
            part = raw[:, group * 8 : (group + 1) * 8, i * 128 : (i + 1) * 128].astype(F32)
            wide32[group, i] = part.reshape(events * 8, 128)

    def turn(k):
        if k * CHUNK % 8 == 0:
            spread(k * CHUNK // 8)
        for c in range(k * CHUNK, (k + 1) * CHUNK):
            for i in range(lanes):
                lane_block = wide32[c // 8, i, pl.ds(c % 8, events, stride=8), :]
                cells[c, events : 2 * events, i * 128 : (i + 1) * 128] = lane_block.astype(BF16)

    back_rows = events * LAGS // 128

    def remote(src, dst, send, recv, peer):
        return pltpu.make_async_remote_copy(
            src_ref=src, dst_ref=dst, send_sem=send, recv_sem=recv,
            device_id=peer, device_id_type=MESH,
        )

    code_copies = [
        remote(codes.at[0], codes.at[slot], code_send.at[slot - 1], code_recv.at[slot - 1], peer)
        for slot, peer in ((2, left), (1, right), (4, up), (3, down))
    ]
    has_from = {1: has_left, 2: has_right, 3: has_up, 4: has_down}

    def traces_low(k, peer):
        block = pl.ds(k * CHUNK, CHUNK)
        return remote(
            cells.at[block, events : 2 * events, :], cells.at[block, 2 * events : 3 * events, :],
            x_send_low.at[k], x_from_high.at[k], peer,
        )

    def traces_high(k, peer):
        block = pl.ds(k * CHUNK, CHUNK)
        return remote(
            cells.at[block, events : 2 * events, :], cells.at[block, 0:events, :],
            x_send_high.at[k], x_from_low.at[k], peer,
        )

    def sums_low(k, peer):
        return remote(sent_low.at[k], got_high.at[k], y_send_low.at[k], y_from_high.at[k], peer)

    def sums_high(k, peer):
        return remote(sent_high.at[k], got_low.at[k], y_send_high.at[k], y_from_low.at[k], peer)

    across = ((has_left, left), (has_right, right))
    along = ((has_up, up), (has_down, down))

    def start(make_low, make_high, k, peers):
        (has_low, low), (has_high, high) = peers
        start_if(has_low, lambda: make_low(k, low))
        start_if(has_high, lambda: make_high(k, high))

    def wait_recv(make_low, make_high, k, peers):
        (has_low, low), (has_high, high) = peers
        wait_recv_if(has_low, lambda: make_high(k, high))
        wait_recv_if(has_high, lambda: make_low(k, low))

    def wait_send(make_low, make_high, k, peers):
        (has_low, low), (has_high, high) = peers
        wait_send_if(has_low, lambda: make_low(k, low))
        wait_send_if(has_high, lambda: make_high(k, high))

    def by_axis(act, make_low, make_high, k, is_across):
        @when(is_across)
        def _():
            act(make_low, make_high, k, across)

        @when(not is_across if isinstance(is_across, bool) else jnp.logical_not(is_across))
        def _():
            act(make_low, make_high, k, along)

    def two_low(k, peer):
        block = pl.ds(k * CHUNK, 2 * CHUNK)
        return remote(
            cells.at[block, events : 2 * events, :], cells.at[block, 2 * events : 3 * events, :],
            x_send_low.at[k], x_from_high.at[k], peer,
        )

    def two_high(k, peer):
        block = pl.ds(k * CHUNK, 2 * CHUNK)
        return remote(
            cells.at[block, events : 2 * events, :], cells.at[block, 0:events, :],
            x_send_high.at[k], x_from_low.at[k], peer,
        )

    def on_traces(act, k):
        @when((k >= HYBRID) & (k < EARLY - 2))
        def _():
            act(traces_low, traces_high, k, across)

        @when(k == EARLY - 2)
        def _():
            act(two_low, two_high, k, across)

        @when((k < HYBRID) | (k >= EARLY))
        def _():
            act(traces_low, traces_high, k, along)

    def on_sums(act, k):
        by_axis(act, sums_low, sums_high, k, k >= EARLY)

    def side_copy(k, n):
        return remote(
            cells.at[k * CHUNK + n, events : 2 * events, :],
            side.at[k, n * events : (n + 1) * events, :],
            side_send.at[k, n], side_recv.at[k, n], (right, left)[n],
        )

    def back_copy(pair, n, rows):
        return remote(
            back_out.at[pair, n, 0:rows, :], back_in.at[pair, n, 0:rows, :],
            back_send.at[pair, n], back_recv.at[pair, n], (left, right)[n],
        )

    def on_back(act, has, k, place):
        @when((k % 2 == place) & (k < HYBRID // 2 * 2))
        def _():
            for n in range(CHUNK):
                act(has[n], lambda: back_copy(k // 2, n, 2 * back_rows + 16))

        if HYBRID % 2:
            @when(k == HYBRID - 1)
            def _():
                for n in range(CHUNK):
                    act(has[n], lambda: back_copy(k // 2, n, back_rows + 16))

    has_target, has_origin = (has_right, has_left), (has_left, has_right)

    def start_if(has, make):
        @pl.when(has)
        def _():
            make().start()

    def wait_send_if(has, make):
        @pl.when(has)
        def _():
            make().wait_send()

    def wait_recv_if(has, make):
        @pl.when(has)
        def _():
            make().wait_recv()

    for load in loads:
        load.wait()
    load_fwd = pltpu.make_async_copy(fwd_hbm, fwd, table_sem.at[0])
    load_inv = pltpu.make_async_copy(inv_hbm, inv, table_sem.at[1])
    load_fwd.start()
    load_inv.start()

    turn(0)
    peers = sum(has.astype(jnp.int32) for has, _ in sides)
    pl.semaphore_wait(barrier, peers)
    for k in range(HYBRID):
        if k > 0:
            turn(k)
        for n in range(CHUNK):
            start_if(has_target[n], lambda: side_copy(k, n))
        if k == 0:
            for copy, (has, _) in zip(code_copies, sides):
                start_if(has, lambda: copy)
        on_traces(start, k)
    for k in range(HYBRID, chunks):
        turn(k)
    for k in range(EARLY, chunks):
        start(traces_low, traces_high, k, along)
    start(traces_low, traces_high, HYBRID, across)

    def blank(has, slot, block, span, first_row, row_count):
        @pl.when(jnp.logical_not(has))
        def _():
            codes[slot] = jnp.full(codes.shape[1:], -1, jnp.int32)

            def clear(n, _):
                block[n, first_row : first_row + row_count, :] = jnp.zeros(
                    (row_count, block.shape[2]), block.dtype
                )
                return 0

            lax.fori_loop(*span, clear, 0)

    hybrid_to, early_to = HYBRID * CHUNK, EARLY * CHUNK
    for span in ((0, hybrid_to), (early_to, channels)):
        blank(has_up, 3, cells, span, 0, events)
        blank(has_down, 4, cells, span, 2 * events, events)
    blank(has_left, 1, cells, (hybrid_to, early_to), 0, events)
    blank(has_right, 2, cells, (hybrid_to, early_to), 2 * events, events)
    blank(has_up, 3, got_low, (0, EARLY), 0, got_low.shape[1])
    blank(has_down, 4, got_high, (0, EARLY), 0, got_high.shape[1])
    blank(has_left, 1, got_low, (EARLY, last), 0, got_low.shape[1])
    blank(has_right, 2, got_high, (EARLY, last), 0, got_high.shape[1])
    blank(has_left, 1, tail_in.at[0], (0, CHUNK), 0, tail_in.shape[2])
    blank(has_right, 2, tail_in.at[1], (0, CHUNK), 0, tail_in.shape[2])
    blank(has_left, 1, side, (0, HYBRID), 0, events)
    blank(has_right, 2, side, (0, HYBRID), events, events)
    for pair in range(back_in.shape[0]):
        blank(has_right, 2, back_in.at[pair], (0, 1), 0, back_in.shape[2])
        blank(has_left, 1, back_in.at[pair], (1, 2), 0, back_in.shape[2])

    for copy, slot, (has, _) in zip(code_copies, (2, 1, 4, 3), sides):
        wait_send_if(has, lambda: copy)
        wait_recv_if(has_from[slot], lambda: copy)

    ids = lax.broadcasted_iota(jnp.int32, (events, slots), 0)

    def ends(slot, heading):
        code = codes[slot, heading : heading + 1, 0:slots]
        live = code >= 0
        head = jnp.where(live, code // events, -1)
        tail = jnp.where(live, code % events, -1)
        return (
            jnp.where(ids == head, 1.0, 0.0).astype(BF16),
            jnp.where(ids == tail, 1.0, 0.0).astype(BF16),
        )

    def outer(a, b):
        return lax.dot_general(
            a, b, (((1,), (1,)), ((), ())), preferred_element_type=F32
        )

    def count(target, target_heading, source, source_heading):
        head, tail = ends(target, target_heading)
        pairs = outer(head, tail)
        head, tail = ends(source, source_heading)
        return (pairs + outer(tail, head)).astype(BF16)

    by_row = {-1: 3, 0: 0, 1: 4}
    by_col = {-1: 1, 0: 0, 1: 2}
    for i in (-1, 0, 1):
        for j in (-1, 0, 1):
            rows_at = pl.ds((i + 1) * events, events)
            weights[0, rows_at, (j + 1) * events : (j + 2) * events] = count(
                by_row[i], (1 - i) * 3 + (j + 1), by_col[j], (i + 1) * 3 + (1 - j)
            )
            weights[1, rows_at, (j + 1) * events : (j + 2) * events] = count(
                by_col[i], (j + 1) * 3 + (1 - i), by_row[j], (1 - j) * 3 + (i + 1)
            )

    load_fwd.wait()
    load_inv.wait()

    size = CHUNK * events

    def diagonal(n):
        at = [lax.broadcasted_iota(jnp.int32, (n, n), dim) for dim in (0, 1)]
        return at[0] == at[1]

    def encoded(part):
        n = part.shape[0]
        peak = jnp.max(jnp.abs(part), axis=1, keepdims=True)
        power = jnp.ceil(jnp.log2(jnp.maximum(peak, 1e-30)) + 1e-4)
        code = jnp.round(part * (jnp.exp2(-power) * CODE_MAX))
        band = jnp.sum(jnp.where(diagonal(n), power, 0.0), axis=0, keepdims=True)
        band = jnp.broadcast_to(band, (16, n)).astype(jnp.int32).astype(jnp.int16)
        return code.astype(jnp.int32).astype(jnp.int16), band

    def encode(ref, at, part):
        n = part.shape[0]
        code, band = encoded(part)
        for i in range(lanes):
            ref[*at, i * n : (i + 1) * n, :] = code[:, i * 128 : (i + 1) * 128]
        ref[*at, lanes * n : lanes * n + 16, 0:n] = band

    def decode(ref, at, n):
        band = ref[*at, lanes * n : lanes * n + 16, 0:n].astype(jnp.int32).astype(F32)[0:1]
        power = jnp.sum(jnp.where(diagonal(n), band, 0.0), axis=1, keepdims=True)
        code = jnp.concatenate(
            [ref[*at, i * n : (i + 1) * n, :] for i in range(lanes)], axis=1
        ).astype(jnp.int32).astype(F32)
        return code * (jnp.exp2(power) * (1.0 / CODE_MAX))

    def gather(k, late):
        on_traces(wait_recv, k)
        parts = [dot(weights[int(late)], cells[k * CHUNK + n]) for n in range(CHUNK)]
        for n in range(CHUNK):
            part_own[k * CHUNK + n] = parts[n][events : 2 * events]
        encode(sent_low, (k,), jnp.concatenate([p[0:events] for p in parts], axis=0))
        encode(sent_high, (k,), jnp.concatenate([p[2 * events :] for p in parts], axis=0))
        start(sums_low, sums_high, k, across if late else along)

    def correlation(x, y):
        size = x.shape[0]
        y_high, y_low = split(y)
        stack = []
        for v in (x, y_high, y_low):
            for i in range(lanes):
                block = v[:, i * BLOCK : (i + 1) * BLOCK]
                stack.append(jnp.concatenate([block, block], axis=1))
        spectra = dot(jnp.concatenate(stack, axis=0), fwd[...])
        spectra = [spectra[n * size : (n + 1) * size] for n in range(3 * lanes)]
        xs = spectra[:lanes]
        ys = [spectra[lanes + i] + spectra[2 * lanes + i] for i in range(lanes)]
        total = jnp.zeros((size, LAGS), F32)
        for n, d in enumerate(SHIFTS):
            real, imag = 0.0, 0.0
            for i in range(max(0, -d), min(lanes, lanes - d)):
                xr, xi = xs[i][:, :BLOCK], xs[i][:, BLOCK:]
                yr, yi = ys[i + d][:, :BLOCK], ys[i + d][:, BLOCK:]
                real = real + (xr * yr + xi * yi)
                imag = imag + (xr * yi - xi * yr)
            s_high, s_low = split(jnp.concatenate([real, imag], axis=1))
            span = slice(n * 2 * BLOCK, (n + 1) * 2 * BLOCK)
            both = dot(jnp.concatenate([s_high, s_low], axis=0), inv[0, span, :])
            total = total + (both[:size] + both[size:] + dot(s_high, inv[1, span, :]))
        return total

    def hybrid_gather(k):
        on_traces(wait_recv, k)
        for n in range(CHUNK):
            wait_recv_if(has_origin[n], lambda: side_copy(k, n))
        c = k * CHUNK
        column_first = dot(weights[1, 0 : 2 * events, :], cells[c])
        column_second = dot(weights[1, events : 3 * events, :], cells[c + 1])
        side_first = dot(weights[0, :, 0:events], side[k, 0:events, :])
        side_second = dot(weights[0, :, 2 * events : 3 * events], side[k, events : 2 * events, :])
        part_own[c] = column_first[events:] + side_first[events : 2 * events]
        part_own[c + 1] = column_second[0:events] + side_second[events : 2 * events]
        encode(sent_low, (k,), jnp.concatenate([side_first[0:events], side_second[0:events]], axis=0))
        encode(
            sent_high, (k,),
            jnp.concatenate([side_first[2 * events :], side_second[2 * events :]], axis=0),
        )
        on_sums(start, k)
        returned = jnp.concatenate([column_first[0:events], column_second[events:]], axis=0)
        code, band = encoded(correlation(side[k], returned))
        pair, half = k // 2, k % 2
        sublane = lax.broadcasted_iota(jnp.int32, (16, size), 0)
        for n in range(CHUNK):
            for i in range(LAGS // 128):
                at = pl.multiple_of(16 + half * back_rows + i * events, 16)
                back_out[pair, n, pl.ds(at, events), :] = code[
                    n * events : (n + 1) * events, i * 128 : (i + 1) * 128
                ]
            before = back_out[pair, n, 0:16, :].astype(jnp.int32)
            back_out[pair, n, 0:16, :] = jnp.where(
                sublane >= 8 * half, band.astype(jnp.int32), before
            ).astype(jnp.int16)
        on_back(start_if, has_origin, k, 1)

    def add_back(k):
        on_back(wait_recv_if, has_target, k, 0)
        pair, half = k // 2, k % 2
        bands = [back_in[pair, n, 0:16, :].astype(jnp.int32).astype(F32) for n in range(CHUNK)]
        lane = lax.broadcasted_iota(jnp.int32, (16, size), 1)
        band = jnp.where(lane < events, bands[0], bands[1])
        band = jnp.where(half == 0, band[0:1], band[8:9])
        power = jnp.sum(jnp.where(diagonal(size), band, 0.0), axis=1, keepdims=True)
        code = jnp.concatenate(
            [
                jnp.concatenate(
                    [
                        back_in[
                            pair, n,
                            pl.ds(
                                pl.multiple_of(16 + half * back_rows + i * events, 16), events
                            ),
                            :,
                        ]
                        for i in range(LAGS // 128)
                    ],
                    axis=1,
                )
                for n in range(CHUNK)
            ],
            axis=0,
        )
        acc[...] += code.astype(jnp.int32).astype(F32) * (jnp.exp2(power) * (1.0 / CODE_MAX))

    def tail_rows(n):
        return pl.ds(0, lanes * events + (16 if n == 0 else 0))

    def tail_low(n):
        return remote(
            tail_out.at[0, n, tail_rows(n)], tail_in.at[1, n, tail_rows(n)],
            tail_send.at[0, n], tail_recv.at[1, n], left,
        )

    def tail_high(n):
        return remote(
            tail_out.at[1, n, tail_rows(n)], tail_in.at[0, n, tail_rows(n)],
            tail_send.at[1, n], tail_recv.at[0, n], right,
        )

    def gather_last():
        wait_recv(traces_low, traces_high, last, along)
        parts = [dot(weights[1], cells[last * CHUNK + n]) for n in range(CHUNK)]
        for n in range(CHUNK):
            part_own[last * CHUNK + n] = parts[n][events : 2 * events]
        for way, first_row in ((0, 0), (1, 2 * events)):
            code, band = encoded(
                jnp.concatenate([p[first_row : first_row + events] for p in parts], axis=0)
            )
            for n in range(CHUNK):
                for i in range(lanes):
                    tail_out[way, n, i * events : (i + 1) * events, :] = code[
                        n * events : (n + 1) * events, i * 128 : (i + 1) * 128
                    ]
            tail_out[way, 0, lanes * events : lanes * events + 16, :] = band
        for n in range(CHUNK):
            start_if(has_left, lambda: tail_low(n))
            start_if(has_right, lambda: tail_high(n))

    def tail_part(way, n):
        band = tail_in[way, 0, lanes * events : lanes * events + 16, :]
        band = band.astype(jnp.int32).astype(F32)[0:1]
        power = jnp.sum(jnp.where(diagonal(size), band, 0.0), axis=1, keepdims=True)
        code = jnp.concatenate(
            [tail_in[way, n, i * events : (i + 1) * events, :] for i in range(lanes)], axis=1
        ).astype(jnp.int32).astype(F32)
        return code * (jnp.exp2(power[n * events : (n + 1) * events]) * (1.0 / CODE_MAX))

    def correlate_last():
        for n in range(CHUNK):
            c = last * CHUNK + n
            wait_recv_if(has_left, lambda: tail_high(n))
            wait_recv_if(has_right, lambda: tail_low(n))
            y = part_own[c] + tail_part(0, n) + tail_part(1, n)
            keep(c, correlation(cells[c, events : 2 * events, :], y))

    def keep(c, rows):
        for i in range(LAGS // 128):
            held[c // 8, i, pl.ds(c % 8, events, stride=8), :] = rows[:, i * 128 : (i + 1) * 128]

    def flush(group):
        place = pl.ds(group * 8, 8)
        for i in range(LAGS // 128):
            out[:, place, i * 128 : (i + 1) * 128] = held[group, i].reshape(events, 8, 128)

    def correlate(k):
        on_sums(wait_recv, k)
        block = pl.ds(k * CHUNK, CHUNK)
        x = cells[block, events : 2 * events, :].reshape(size, samples)
        y = part_own[block].reshape(size, samples) + decode(got_low, (k,), size) + decode(got_high, (k,), size)
        acc[...] = correlation(x, y)

        @pl.when(k < HYBRID)
        def _():
            add_back(k)

        total = acc[...]
        for n in range(CHUNK):
            keep(k * CHUNK + n, total[n * events : (n + 1) * events])

    def finish(k):
        on_traces(wait_send, k)

        @when(k < last)
        def _():
            on_sums(wait_send, k)

        @when(k < HYBRID)
        def _():
            for n in range(CHUNK):
                wait_send_if(has_target[n], lambda: side_copy(k, n))
            on_back(wait_send_if, has_origin, k, 1)

    def step(k, _):
        ahead = k + AHEAD

        @pl.when(k == 2)
        def _():
            start(two_low, two_high, EARLY - 2, across)

        @pl.when(k < HYBRID)
        def _():
            hybrid_gather(k)

        @pl.when((k >= HYBRID) & (k < EARLY))
        def _():
            gather(k, False)

        @pl.when((ahead >= EARLY) & (ahead < last))
        def _():
            gather(ahead, True)

        @pl.when(ahead == last)
        def _():
            gather_last()

        place = k - LAG
        moved = (place >= HYBRID) & (place < HYBRID + FORWARD)
        held_back = (place >= HYBRID + FORWARD) & (place < EARLY + FORWARD)

        @pl.when((place >= 0) & (place < last))
        def _():
            correlate(
                place
                + (EARLY - HYBRID) * moved.astype(jnp.int32)
                - FORWARD * held_back.astype(jnp.int32)
            )

        @pl.when(place == last - 1)
        def _():
            for group in range(channels // 8 - 1):
                flush(group)

        @pl.when(k >= SETTLE)
        def _():
            finish(k - SETTLE)

        return 0

    lax.fori_loop(0, last + LAG, step, 0)
    for k in range(last + LAG - SETTLE, chunks):
        finish(k)
    correlate_last()
    flush(channels // 8 - 1)
    for n in range(CHUNK):
        wait_send_if(has_left, lambda: tail_low(n))
        wait_send_if(has_right, lambda: tail_high(n))


def by_heading(pairs):
    return pairs.transpose(0, 2, 1, 3)[0]


def local(forward, inverse, traces, pair_first, pair_second, pair_valid):
    _, _, events, channels, samples = traces.shape
    chunks = channels // CHUNK
    part = pltpu.VMEM((channels, events, samples), F32)
    code = pltpu.VMEM((chunks, CHUNK * events * samples // 128 + 16, 128), jnp.int16)
    pairs = -(-HYBRID // 2)
    back = pltpu.VMEM((pairs, CHUNK, 2 * events * LAGS // 128 + 16, 128), jnp.int16)
    tail = pltpu.VMEM((2, CHUNK, events * samples // 128 + 16, 128), jnp.int16)
    in_hbm = pl.BlockSpec(memory_space=pltpu.HBM)
    in_vmem = pl.BlockSpec(memory_space=pltpu.VMEM)
    dma = pltpu.SemaphoreType.DMA
    out = pl.pallas_call(
        kernel,
        out_shape=jax.ShapeDtypeStruct((events, channels, LAGS), F32),
        in_specs=[in_hbm, in_vmem, in_vmem, in_vmem, in_hbm, in_hbm],
        out_specs=in_vmem,
        scratch_shapes=[
            pltpu.VMEM((events, channels, samples), BF16),
            pltpu.VMEM((channels // 8, samples // 128, events * 8, 128), F32),
            pltpu.VMEM((channels, 3 * events, samples), BF16),
            part, code, code, code, code,
            pltpu.VMEM((HYBRID, CHUNK * events, samples), BF16),
            back, back, tail, tail,
            pltpu.VMEM((CHUNK * events, LAGS), F32),
            pltpu.VMEM((2, 3 * events, 3 * events), BF16),
            pltpu.VMEM((5, 16, 128), jnp.int32),
            pltpu.VMEM(forward.shape, BF16),
            pltpu.VMEM(inverse.shape, BF16),
            pltpu.VMEM((channels // 8, LAGS // 128, events * 8, 128), F32),
            dma((LOADS,)), dma((2,)), dma((4,)), dma((4,)),
        ] + [dma((chunks,))] * 8 + [dma((HYBRID, CHUNK))] * 2 + [dma((pairs, CHUNK))] * 2 + [dma((2, CHUNK))] * 2,
        compiler_params=pltpu.CompilerParams(
            collective_id=0, has_side_effects=True, vmem_limit_bytes=40 * 1024 * 1024
        ),
        cost_estimate=pl.CostEstimate(
            flops=8 * 10**9, bytes_accessed=6 * 10**6, transcendentals=0
        ),
        name="event_correlation",
    )(*[pltpu.with_memory_space_constraint(v, pltpu.HBM) for v in (traces[0, 0], by_heading(pair_first), by_heading(pair_second), by_heading(pair_valid), forward, inverse)])
    return out[None, None]


def solution(mesh):
    forward, inverse = make_tables(512)
    spec4 = P("wide", "narrow", None, None)
    spec5 = P("wide", "narrow", None, None, None)

    def run(traces, pair_first, pair_second, pair_valid):
        return local(
            jnp.asarray(forward), jnp.asarray(inverse), traces, pair_first, pair_second, pair_valid
        )

    return jax.shard_map(
        run, mesh=mesh, in_specs=(spec5, spec4, spec4, spec4), out_specs=spec5, check_vma=False
    )
```
